32 devices in a mesh: sector: 4 (over x, core), section: 8 (over z, y).
Axes of the slice: x: 2, y: 2, z: 4, core: 2. Of those that a mesh axis runs over, the one named last changes fastest.
Arguments:
- vectors: bfloat16 [12288, 512], P(('sector', 'section')), may hold values from -6 to 6
- sectors: int32 [12288, 2], P(('sector', 'section')), may hold values from 0 to 15, all different within a row; in each aligned block of 384 rows (0 to 383, 384 to 767, ...) at most 72 rows name the same one
- outcomes: int32 [12288, 2], P(('sector', 'section')), may hold values from 0 to 3
- sites: bfloat16 [2, 16, 512, 2048], P(None, 'sector'), may hold values from -0.25 to 0.25
- environments: bfloat16 [2, 16, 4, 512, 512], P(None, 'sector', None, 'section'), may hold values from -100 to 150, as said below
Outputs:
- probabilities: bfloat16 [12288, 8], P(('sector', 'section'))
- final_vectors: bfloat16 [12288, 512], P(('sector', 'section'))
The draws below stay inside these ranges and needn't reach their ends.
Inputs may be any that keep to these rules, and one draw needn't show every extreme that they name: `sectors`: in the rows of one device no sector appears more than 72 times over all orbitals together, and on some device some sector appears exactly 72 times. Every block environments[k, q, s] is symmetric and positive definite.
All inputs are finite; a program needn't handle non-finite values.
Results may differ from the reference program's by a relative error of at most 0.0049.
Values may be sent and summed in bfloat16 or wider, within the bound.
A program may use at most 128 MiB of HBM per device.

```python
import math
import jax
import jax.numpy as jnp
import numpy as np
from jax import lax

B = 512
OUTCOMES = 4
ORBITALS = 2
SMP_DEV = 384
NSEC = 16
SAMPLES = 12288
CAP = 72


def draw_environments(key, part):
    key_dense = jax.random.fold_in(key, 11)
    key_scale = jax.random.fold_in(key, 13)
    shape = (ORBITALS, NSEC, OUTCOMES, B, B)
    index = jnp.arange(B)
    dense = jax.random.normal(key_dense, shape, jnp.float32)
    dense = jnp.where((index == 1)[:, None], -dense[..., 0:1, :], dense)
    dense = dense / jnp.sqrt(jnp.sum(dense * dense, axis=-1, keepdims=True))
    core = jnp.einsum('...ij,...kj->...ik', dense, dense, precision=lax.Precision.HIGHEST)
    identity = (index[:, None] == index[None, :]).astype(jnp.float32)
    core = core + 0.5 * identity
    top_level = 0.5 * math.log(10.0)
    levels = jax.random.uniform(key_scale, shape[:-1], jnp.float32, 0.0, top_level)
    levels = jnp.where(index < 2, top_level, levels)
    spread = jnp.exp(levels)
    return (spread[..., :, None] * core * spread[..., None, :]).astype(jnp.bfloat16)


def set_ends(entries, key, smallest, largest):
    place = [jax.random.randint(jax.random.fold_in(key, axis), (), 0, length) for axis, length in enumerate(entries.shape)]
    main_axis = entries.shape.index(max(entries.shape))
    next_to = place[:main_axis] + [(place[main_axis] + 1) % entries.shape[main_axis]] + place[main_axis + 1:]
    return entries.at[tuple(place)].set(smallest).at[tuple(next_to)].set(largest)


def block_scale(rng, shape, split, low, largest):
    factor_of = 1.0
    for dim, blocks in split:
        draws = jax.random.uniform(jax.random.fold_in(jax.random.fold_in(rng, 6), dim), (blocks,), jnp.float32, low / len(split), largest / len(split))
        factor_of = factor_of * jnp.repeat(jnp.exp(draws), shape[dim] // blocks).reshape((-1,) + (1,) * (len(shape) - 1 - dim))
    return factor_of


def shared_out(key, own, number, rows, count, top, bound, lean):
    sequence = jax.random.permutation(key, count)
    crowded, ordinary = shares(count, rows * top, bound, lean, True), shares(count, rows * top, bound, lean, False)
    places = jnp.arange(count)

    def named(lengths, offset_by):
        used = int((lengths > 0).sum())
        fixed = max(1, used // 4)
        moved = fixed + (places - fixed + offset_by * (used - fixed)) % max(1, count - fixed)
        return jnp.zeros((count,), jnp.int32).at[sequence[jnp.where(places < fixed, places, moved)]].set(jnp.asarray(lengths, jnp.int32))

    lengths = jnp.where(number % 4 == 0, named(crowded, number // 4), named(ordinary, number - number // 4 - 1))
    mixed = jax.random.permutation(jax.random.fold_in(own, 3), count)
    donor, receiver = mixed[0:count // 2 * 2:2], mixed[1:count // 2 * 2:2]
    margin = jnp.minimum(lengths[donor] - 1, bound - lengths[receiver]) // 2
    margin = jnp.where((donor == sequence[0]) | (receiver == sequence[0]) | (lengths[receiver] == 0), 0, jnp.maximum(margin, 0))
    moved = jax.random.randint(jax.random.fold_in(own, 4), (count // 2,), 0, 1 << 20) % (margin + 1)
    lengths = lengths.at[donor].add(-moved).at[receiver].add(moved)
    items = jnp.searchsorted(jnp.cumsum(lengths), jnp.arange(rows * top), side="right").astype(jnp.int32)
    listing = items.reshape(top, rows).T
    listing = listing[jax.random.permutation(jax.random.fold_in(own, 1), rows)]
    offset_by = jax.random.randint(jax.random.fold_in(own, 2), (rows, 1), 0, top)
    return jnp.take_along_axis(listing, (jnp.arange(top)[None, :] + offset_by) % top, axis=1)


def shares(amount, total, reach, lean, full):
    weights = [(1 << 20) // math.isqrt(standing ** lean) + 1 for standing in range(1, amount + 1)]
    largest = reach if full else min(reach, max(-(-total // amount), total * weights[0] // sum(weights)))
    least = 1 if total - largest >= amount - 1 else 0
    counts, rest = [largest] + [least] * (amount - 1), total - largest - least * (amount - 1)
    while rest > 0:
        movable = [i for i in range(1, amount) if counts[i] < largest] or [i for i in range(1, amount) if counts[i] < reach]
        pool, remaining = sum([weights[i] for i in movable]), rest
        for i in movable:
            addition = min(reach - counts[i], max(1, remaining * weights[i] // pool), rest)
            counts[i] = counts[i] + addition
            rest = rest - addition
    return np.array(counts)


def gaussian(own_key, dims, deviation, most, cuts=(), kind=jnp.bfloat16):
    drawn = deviation * jax.random.normal(own_key, dims, jnp.float32)
    if cuts:
        drawn = drawn * block_scale(own_key, dims, cuts, -0.22, 0.18)
    return jnp.clip(drawn, -most, most).astype(kind)


def setup_inputs(seed: int = 0) -> dict:
    keys = jax.random.split(jax.random.key(seed), 6)
    vectors = gaussian(keys[0], (SAMPLES, B), 1.0, 6.0, ((0, 32),))
    sectors_keys = jax.random.split(jax.random.fold_in(keys[1], 1), SAMPLES // SMP_DEV)
    sectors_turns = jax.random.permutation(jax.random.fold_in(keys[1], 3), SAMPLES // SMP_DEV)
    sectors = jax.vmap(lambda own, number: shared_out(jax.random.fold_in(keys[1], 2), own, number, SMP_DEV, NSEC, ORBITALS, CAP, 2))(sectors_keys, sectors_turns).reshape((SAMPLES, ORBITALS))
    outcomes = set_ends(jax.random.randint(keys[2], (SAMPLES, ORBITALS), 0, OUTCOMES), jax.random.fold_in(keys[2], 1), 0, OUTCOMES - 1).astype(jnp.int32)
    sites = gaussian(keys[3], (ORBITALS, NSEC, B, OUTCOMES * B), B ** -0.5, 0.25, ((1, 4),))
    environments = draw_environments(jax.random.fold_in(keys[5], 71), 0)
    return dict(vectors=vectors, sectors=sectors, outcomes=outcomes, sites=sites, environments=environments)


def orbital_pass(current, labels, chosen_ids, site_k, environ_k):
    sample_total = labels.shape[0]
    block_size = math.gcd(sample_total, 256)
    block_count = sample_total // block_size
    ordering = jnp.argsort(labels, stable=True).astype(jnp.int32)
    sorted_labels = labels[ordering]
    sorted_rows = current[ordering]
    sorted_ids = chosen_ids[ordering]

    def process_block(pieces):
        block_rows, block_labels, block_ids = pieces
        lowest = block_labels[0]
        highest = block_labels[-1]
        start_pair = (jnp.zeros((block_size, OUTCOMES), jnp.bfloat16), jnp.zeros((block_size, B), jnp.bfloat16))

        def sector_step(sector_id, carry_pair):
            amplitudes = jnp.dot(block_rows, site_k[sector_id], preferred_element_type=jnp.float32)
            amplitudes = amplitudes.reshape(block_size, OUTCOMES, B)
            rounded = lax.optimization_barrier(amplitudes.astype(jnp.bfloat16)).astype(jnp.float32)
            images = jnp.einsum('rsb,sbe->rse', rounded, environ_k[sector_id].astype(jnp.float32))
            weights = lax.optimization_barrier(jnp.sum(images * amplitudes, axis=-1))
            norm_sum = lax.optimization_barrier(jnp.sum(weights, axis=-1))
            branch_probs = (weights / norm_sum[:, None]).astype(jnp.bfloat16)
            chosen_mask = (block_ids[:, None] == jnp.arange(OUTCOMES, dtype=jnp.int32)[None, :]).astype(jnp.float32)
            chosen_weight = lax.optimization_barrier(jnp.sum(chosen_mask * weights, axis=-1))
            picked = lax.optimization_barrier(jnp.sum(chosen_mask[:, :, None] * amplitudes, axis=1))
            advanced = (picked * lax.rsqrt(chosen_weight / B)[:, None]).astype(jnp.bfloat16)
            inside = (block_labels == sector_id)[:, None]
            return (jnp.where(inside, branch_probs, carry_pair[0]), jnp.where(inside, advanced, carry_pair[1]))
        return lax.fori_loop(lowest, highest + 1, sector_step, start_pair)
    probs_sorted, rows_sorted = lax.map(process_block, (sorted_rows.reshape(block_count, block_size, B), sorted_labels.reshape(block_count, block_size), sorted_ids.reshape(block_count, block_size)))
    branch_probs = jnp.zeros((sample_total, OUTCOMES), jnp.bfloat16).at[ordering].set(probs_sorted.reshape(sample_total, OUTCOMES))
    advanced = jnp.zeros((sample_total, B), jnp.bfloat16).at[ordering].set(rows_sorted.reshape(sample_total, B))
    return (branch_probs, advanced)

def reference(vectors, sectors, outcomes, sites, environments):
    current = vectors
    columns = []
    for orbital in range(ORBITALS):
        branch_probs, current = orbital_pass(current, sectors[:, orbital], outcomes[:, orbital], sites[orbital], environments[orbital])
        columns.append(branch_probs)
    return (jnp.concatenate(columns, axis=1), current)
```

```python
import jax
import jax.numpy as jnp
from jax import lax
from jax.sharding import Mesh, PartitionSpec as P

OUTCOMES = 4
ORBITALS = 2


def slot_positions(labels, sector_total):
    onehot = (labels[:, None] == jnp.arange(sector_total, dtype=jnp.int32)[None, :]).astype(
        jnp.bfloat16
    )
    count = labels.shape[0]
    lower = (jnp.arange(count)[:, None] > jnp.arange(count)[None, :]).astype(jnp.bfloat16)
    before = jnp.dot(lower, onehot, preferred_element_type=jnp.float32)
    return jnp.sum(before * onehot.astype(jnp.float32), axis=1).astype(jnp.int32)


def local(vectors, sectors, outcomes, sites, environments):
    per_device = sites.shape[1]
    sector_total = per_device * lax.axis_size("sector")
    sample_count, width = vectors.shape
    capacity = max(2, (3 * sample_count + sector_total - 1) // sector_total)
    slots = sector_total * capacity
    own = lax.axis_index("own")
    peers = ("sector", "own")

    environ = []
    for k in range(ORBITALS):
        part = lax.all_to_all(environments[k], "own", split_axis=0, concat_axis=0, tiled=True)
        whole = lax.all_gather(part, "grp", axis=0, tiled=True)
        whole = jnp.transpose(whole, (1, 0, 2, 3)).reshape(OUTCOMES, width, width)
        environ.append(whole)

    hots = []
    ids = []
    for k in range(ORBITALS):
        labels = sectors[:, k]
        slot_of = labels * capacity + slot_positions(labels, sector_total)
        hot = (jnp.arange(slots, dtype=jnp.int32)[:, None] == slot_of[None, :])
        hots.append(hot.astype(jnp.bfloat16))
        ids.append(jnp.sum(jnp.where(hot, outcomes[:, k][None, :] + 1, 0), axis=1) - 1)
    send_ids = jnp.stack(ids, 0).reshape(ORBITALS, sector_total, capacity).transpose(1, 0, 2)
    ids_in = lax.all_to_all(send_ids.astype(jnp.bfloat16), peers, split_axis=0, concat_axis=0, tiled=True)
    ids_in = ids_in.astype(jnp.float32)

    current = vectors
    probs_out = []
    for k in range(ORBITALS):
        hot = hots[k]
        rows = jnp.dot(hot, current, preferred_element_type=jnp.float32).astype(jnp.bfloat16)
        rows = rows.reshape(sector_total, capacity, width)
        rows_in = lax.all_to_all(rows, peers, split_axis=0, concat_axis=0, tiled=True)
        rows_in = rows_in.reshape(slots, width)
        site = lax.dynamic_index_in_dim(sites[k], own, 0, keepdims=False)
        chosen = ids_in[:, k, :].reshape(slots)
        weights = []
        picked = jnp.zeros((slots, width), jnp.float32)
        for s in range(OUTCOMES):
            amp = jnp.dot(rows_in, site[:, s * width : (s + 1) * width], preferred_element_type=jnp.float32)
            image = jnp.dot(amp.astype(jnp.bfloat16), environ[k][s], preferred_element_type=jnp.float32)
            weights.append(jnp.sum(image * amp, axis=-1))
            picked = jnp.where((chosen == s)[:, None], amp, picked)
        filled = chosen >= 0.0
        weights = jnp.stack(weights, 0)
        total = jnp.sum(weights, axis=0)
        probs = (weights / jnp.where(filled, total, 1.0)[None, :]).astype(jnp.bfloat16)
        probs_out.append(jnp.where(filled[None, :], probs, 0))
        mask = chosen[None, :] == jnp.arange(OUTCOMES, dtype=jnp.float32)[:, None]
        weight = jnp.sum(jnp.where(mask, weights, 0.0), axis=0)
        scale = lax.rsqrt(jnp.where(filled, weight, 1.0) / width)
        advanced = (picked * scale[:, None]).astype(jnp.bfloat16)
        back = lax.all_to_all(
            advanced.reshape(sector_total, capacity, width), peers, split_axis=0, concat_axis=0, tiled=True
        ).reshape(slots, width)
        current = lax.dot_general(
            hot, back, (((0,), (0,)), ((), ())), preferred_element_type=jnp.float32
        ).astype(jnp.bfloat16)
    probs = jnp.stack(probs_out, 0).reshape(ORBITALS * OUTCOMES, sector_total, capacity)
    probs = lax.all_to_all(probs.transpose(1, 0, 2), peers, split_axis=0, concat_axis=0, tiled=True)
    probs = probs.transpose(0, 2, 1).reshape(slots, ORBITALS, OUTCOMES)
    columns = []
    for k in range(ORBITALS):
        columns.append(
            lax.dot_general(hots[k], probs[:, k], (((0,), (0,)), ((), ())), preferred_element_type=jnp.float32)
        )
    return jnp.concatenate(columns, axis=1).astype(jnp.bfloat16), current


def solution(mesh):
    def run(vectors, sectors, outcomes, sites, environments):
        sector_size, section_size = mesh.devices.shape
        owners = sites.shape[1] // sector_size
        split = Mesh(
            mesh.devices.reshape(sector_size, section_size // owners, owners), ("sector", "grp", "own")
        )
        every = P(("sector", "grp", "own"), None)
        return jax.shard_map(
            local,
            mesh=split,
            in_specs=(
                every,
                every,
                every,
                P(None, "sector", None, None),
                P(None, "sector", None, ("grp", "own"), None),
            ),
            out_specs=(every, every),
            check_vma=False,
        )(vectors, sectors, outcomes, sites, environments)

    return run
```

```python
import functools

import jax
import jax.numpy as jnp
from jax import lax
from jax.experimental import pallas as pl
from jax.experimental.pallas import tpu as pltpu
from jax.sharding import Mesh, PartitionSpec as P

OUTCOMES = 4
ORBITALS = 2
LANES = 128
CHUNKS = 4
MESH = pl.DeviceIdType.MESH
F32 = jnp.float32
BF16 = jnp.bfloat16


def kernel(
    sizes,
    vec_ref, sec_ref, out_ref, sec_t_ref, site_ref, env_ref,
    prob_ref, fin_ref,
    fs0, fr0, fs1, fr1, rs0, rr0, rs1, rr1,
    site_v, env_in, env_w, hot_t, kept,
    site_sem, fsend, frecv, rsend, rrecv, esend, erecv,
):
    n_sec, n_grp, n_own, cap = sizes
    n = n_sec * n_own
    n_row = n_grp * n_own
    samples, width = vec_ref.shape
    depth = env_ref.shape[3]
    blocks = width // LANES
    per_block = LANES // depth
    per_chunk = n // CHUNKS
    rows = per_chunk * cap
    fs, fr, rs, rr = (fs0, fs1), (fr0, fr1), (rs0, rs1), (rr0, rr1)

    si, gi, oi = lax.axis_index("sector"), lax.axis_index("grp"), lax.axis_index("own")
    me = si * n_own + oi
    row_me = gi * n_own + oi

    def peer(pos):
        pos = lax.rem(pos, n)
        return (lax.div(pos, n_own), gi, lax.rem(pos, n_own))

    def row_peer(pos):
        pos = lax.rem(pos, n_row)
        return (si, lax.div(pos, n_own), lax.rem(pos, n_own))

    def loop(low, high, body):
        lax.fori_loop(low, high, lambda i, c: (body(i), c)[1], 0)

    site_copies = [
        pltpu.make_async_copy(site_ref.at[k, oi], site_v.at[k], site_sem.at[k]) for k in range(ORBITALS)
    ]
    for copy in site_copies:
        copy.start()

    barrier = pltpu.get_barrier_semaphore()

    def greet(r):
        pl.semaphore_signal(barrier, inc=1, device_id=peer(me + r), device_id_type=MESH)

    def greet_far(j):
        pl.semaphore_signal(
            barrier,
            inc=1,
            device_id=(si, lax.rem(gi + 1 + lax.div(j, n_own), n_grp), lax.rem(j, n_own)),
            device_id_type=MESH,
        )

    loop(1, n, greet)
    loop(0, (n_grp - 1) * n_own, greet_far)

    def env_part(k, origin, t):
        column = lax.rem(lax.div(origin, per_block) + t, blocks) * LANES
        return env_in.at[
            k, :, pl.ds(pl.multiple_of(origin * depth, depth), depth), pl.ds(pl.multiple_of(column, LANES), LANES)
        ]

    def has_third(origin):
        m = lax.div(origin, per_block)
        return jnp.logical_or(m == 0, m == blocks - 1)

    def env_copy(k, d, t):
        target = row_peer(row_me + d)
        column = lax.rem(lax.div(row_me, per_block) + t, blocks) * LANES
        return pltpu.make_async_remote_copy(
            src_ref=env_ref.at[k, target[2], :, :, pl.ds(pl.multiple_of(column, LANES), LANES)],
            dst_ref=env_part(k, row_me, t),
            send_sem=esend.at[k, d, t],
            recv_sem=erecv.at[k, d, t],
            device_id=target,
            device_id_type=MESH,
        )

    def env_own(k, t):
        column = lax.rem(lax.div(row_me, per_block) + t, blocks) * LANES
        return pltpu.make_async_copy(
            env_ref.at[k, oi, :, :, pl.ds(pl.multiple_of(column, LANES), LANES)],
            env_part(k, row_me, t),
            erecv.at[k, 0, t],
        )

    def env_arrival(k, d, t):
        origin = lax.rem(row_me - d + n_row, n_row)
        part = env_part(k, origin, t)
        return pltpu.make_async_remote_copy(
            src_ref=part,
            dst_ref=part,
            send_sem=esend.at[k, d, t],
            recv_sem=erecv.at[k, d, t],
            device_id=row_peer(row_me + d),
            device_id_type=MESH,
        )

    def env_start(k):
        def one(d):
            env_copy(k, d, 0).start()
            env_copy(k, d, 1).start()

            @pl.when(has_third(row_me))
            def _():
                env_copy(k, d, 2).start()

        env_own(k, 0).start()
        env_own(k, 1).start()

        @pl.when(has_third(row_me))
        def _():
            env_own(k, 2).start()

        loop(1, n_row, one)

    def env_wait(k):
        def one(d):
            env_arrival(k, d, 0).wait_recv()
            env_arrival(k, d, 1).wait_recv()

            @pl.when(has_third(lax.rem(row_me - d + n_row, n_row)))
            def _():
                env_arrival(k, d, 2).wait_recv()

        env_own(k, 0).wait()
        env_own(k, 1).wait()

        @pl.when(has_third(row_me))
        def _():
            env_own(k, 2).wait()

        loop(1, n_row, one)

    def env_sent(k):
        def one(d):
            env_copy(k, d, 0).wait_send()
            env_copy(k, d, 1).wait_send()

            @pl.when(has_third(row_me))
            def _():
                env_copy(k, d, 2).wait_send()

        loop(1, n_row, one)

    def env_build(k):
        for m in range(blocks):
            for t in range(3 if m in (0, blocks - 1) else 2):
                c = (m + t) % blocks
                at = (slice(m * LANES, (m + 1) * LANES), slice(c * LANES, (c + 1) * LANES))
                part = env_in[k, :, at[0], at[1]]
                env_w[:, at[0], at[1]] = part if t == 0 else part + part

    def relative(labels):
        shifted = labels - me
        return jnp.where(shifted < 0, shifted + n, shifted).astype(F32)

    first = lax.broadcasted_iota(jnp.int32, (samples, samples), 0)
    second = lax.broadcasted_iota(jnp.int32, (samples, samples), 1)
    upper = (first < second).astype(F32).astype(BF16)
    lower = (first > second).astype(F32).astype(BF16)
    slot_rows = []
    marks = []
    lane = lax.broadcasted_iota(jnp.int32, (samples, LANES), 1)
    slot_lane = lax.broadcasted_iota(jnp.int32, (samples, n * cap), 1).astype(F32)
    for k in range(ORBITALS):
        label = relative(sec_t_ref[k : k + 1, :])
        hot = (lax.broadcasted_iota(jnp.int32, (n, samples), 0).astype(F32) == label).astype(F32)
        before = jnp.dot(hot.astype(BF16), upper, preferred_element_type=F32)
        slot_rows.append(label * cap + jnp.sum(before * hot, axis=0, keepdims=True))
        label = relative(sec_ref[:, k : k + 1])
        hot = (lane.astype(F32) == label).astype(F32)
        before = jnp.dot(lower, hot.astype(BF16), preferred_element_type=F32)
        slot = label * cap + jnp.sum(before * hot, axis=1, keepdims=True)
        hot_t[k] = (slot_lane == slot).astype(F32).astype(BF16)
        marks.append((lane == out_ref[:, k : k + 1] + OUTCOMES * k).astype(F32).astype(BF16))

    env_w[...] = jnp.zeros_like(env_w)

    pl.semaphore_wait(barrier, n - 1 + (n_grp - 1) * n_own)

    def piece(ref, r):
        return ref.at[pl.ds(pl.multiple_of(r * cap, 16), cap)]

    def out_copy(k, r):
        return pltpu.make_async_remote_copy(
            src_ref=piece(fs[k], r),
            dst_ref=piece(fr[k], r),
            send_sem=fsend.at[k, r],
            recv_sem=frecv.at[k, r],
            device_id=peer(me + r),
            device_id_type=MESH,
        )

    def back_copy(k, r):
        return pltpu.make_async_remote_copy(
            src_ref=piece(rs[k], r),
            dst_ref=piece(rr[k], r),
            send_sem=rsend.at[k, r],
            recv_sem=rrecv.at[k, r],
            device_id=peer(me - r + n),
            device_id_type=MESH,
        )

    def in_chunk(c, act):
        def one(r):
            @pl.when(r > 0)
            def _():
                act(r)

        loop(c * per_chunk, (c + 1) * per_chunk, one)

    def span(c):
        return pl.ds(pl.multiple_of(c * rows, 16), rows)

    current = vec_ref[...]
    for k in range(ORBITALS):

        def pack(c, k=k, current=current):
            place = (lax.broadcasted_iota(jnp.int32, (rows, samples), 0) + c * rows).astype(F32)
            hot = (place == slot_rows[k]).astype(F32).astype(BF16)
            packed = jnp.dot(hot, current, preferred_element_type=F32).astype(BF16)
            fs[k][span(c), :width] = packed
            if k == 0:
                other = (place == slot_rows[1]).astype(F32).astype(BF16)
                mark = jnp.dot(hot, marks[0], preferred_element_type=F32)
                mark = mark + jnp.dot(other, marks[1], preferred_element_type=F32)
                fs[0][span(c), width:] = mark.astype(BF16)
            in_chunk(c, lambda r: out_copy(k, r).start())

        loop(0, CHUNKS, pack)
        fr[k][:cap] = fs[k][:cap]
        if k == 0:
            env_start(0)
        site_copies[k].wait()
        env_wait(k)
        env_build(k)
        if k == 0:
            env_start(1)

        def work(c, k=k):
            in_chunk(c, lambda r: out_copy(k, r).wait_recv())
            left = fr[k][span(c), :width]
            mark = fr[0][span(c), width:].astype(F32)
            weights = []
            chosen = []
            picked = jnp.zeros((rows, width), F32)
            for s in range(OUTCOMES):
                amp = jnp.dot(left, site_v[k, :, s * width : (s + 1) * width], preferred_element_type=F32)
                image = jnp.dot(amp.astype(BF16), env_w[s], preferred_element_type=F32)
                weights.append(jnp.sum(image * amp, axis=1, keepdims=True))
                at = OUTCOMES * k + s
                chosen.append(mark[:, at : at + 1])
                picked = jnp.where(chosen[s] > 0.0, amp, picked)
            total = weights[0] + weights[1] + weights[2] + weights[3]
            filled = (chosen[0] + chosen[1] + chosen[2] + chosen[3]) > 0.0
            weight = jnp.zeros_like(total)
            for s in range(OUTCOMES):
                weight = jnp.where(chosen[s] > 0.0, weights[s], weight)
            total = jnp.where(filled, total, 1.0)
            scale = lax.rsqrt(jnp.where(filled, weight, 1.0) / width)
            rs[k][span(c), :width] = (picked * scale).astype(BF16)
            lanes = lax.broadcasted_iota(jnp.int32, (rows, LANES), 1)
            probs = jnp.zeros((rows, LANES), F32) if k == 0 else kept[span(c), :].astype(F32)
            for s in range(OUTCOMES):
                value = jnp.where(filled, weights[s] / total, 0.0)
                probs = jnp.where(lanes == OUTCOMES * k + s, value, probs)
            if k == 0:
                kept[span(c), :] = probs.astype(BF16)
            else:
                rs[1][span(c), width:] = probs.astype(BF16)
            in_chunk(c, lambda r: back_copy(k, r).start())

        loop(0, CHUNKS, work)
        rr[k][:cap] = rs[k][:cap]
        loop(1, n, lambda r, k=k: back_copy(k, r).wait_recv())
        current = jnp.dot(hot_t[k], rr[k][:, :width], preferred_element_type=F32).astype(BF16)
    fin_ref[...] = current
    tail = rr[1][:, width:]
    low = jnp.dot(hot_t[0], tail, preferred_element_type=F32)
    high = jnp.dot(hot_t[1], tail, preferred_element_type=F32)
    prob_ref[...] = jnp.where(lane < OUTCOMES, low, high)[:, : OUTCOMES * ORBITALS].astype(BF16)

    for k in range(ORBITALS):
        loop(1, n, lambda r, k=k: out_copy(k, r).wait_send())
        loop(1, n, lambda r, k=k: back_copy(k, r).wait_send())
        env_sent(k)


def local(sizes, vectors, sectors, outcomes, sites, environments):
    n_sec, n_grp, n_own, cap = sizes
    n, n_row = n_sec * n_own, n_grp * n_own
    samples, width = vectors.shape
    slots = n * cap
    vmem = pl.BlockSpec(memory_space=pltpu.VMEM)
    hbm = pl.BlockSpec(memory_space=pl.ANY)
    dma = pltpu.SemaphoreType.DMA
    wide, plain = pltpu.VMEM((slots, width + LANES), BF16), pltpu.VMEM((slots, width), BF16)
    return pl.pallas_call(
        functools.partial(kernel, sizes),
        out_shape=(
            jax.ShapeDtypeStruct((samples, ORBITALS * OUTCOMES), BF16),
            jax.ShapeDtypeStruct((samples, width), BF16),
        ),
        in_specs=[vmem, vmem, vmem, vmem, hbm, hbm],
        out_specs=(vmem, vmem),
        scratch_shapes=[
            wide, wide, plain, plain, plain, plain, wide, wide,
            pltpu.VMEM((ORBITALS, width, OUTCOMES * width), BF16),
            pltpu.VMEM((ORBITALS, OUTCOMES, width, width), BF16),
            pltpu.VMEM((OUTCOMES, width, width), BF16),
            pltpu.VMEM((ORBITALS, samples, slots), BF16),
            pltpu.VMEM((slots, LANES), BF16),
            dma((ORBITALS,)),
            dma((ORBITALS, n)), dma((ORBITALS, n)), dma((ORBITALS, n)), dma((ORBITALS, n)),
            dma((ORBITALS, n_row, 3)), dma((ORBITALS, n_row, 3)),
        ],
        compiler_params=pltpu.CompilerParams(
            collective_id=0, has_side_effects=True, vmem_limit_bytes=56 * 1024 * 1024
        ),
    )(vectors, sectors, outcomes, sectors.T, sites, environments)


def solution(mesh):
    def run(vectors, sectors, outcomes, sites, environments):
        sector_size, section_size = mesh.devices.shape
        owners = sites.shape[1] // sector_size
        split = Mesh(
            mesh.devices.reshape(sector_size, section_size // owners, owners), ("sector", "grp", "own")
        )
        every = P(("sector", "grp", "own"), None)
        per_device = vectors.shape[0] // mesh.devices.size
        cap = -(-3 * per_device // sites.shape[1])
        cap = -(-cap // 16) * 16
        return jax.shard_map(
            functools.partial(local, (sector_size, section_size // owners, owners, cap)),
            mesh=split,
            in_specs=(
                every,
                every,
                every,
                P(None, "sector", None, None),
                P(None, "sector", None, ("grp", "own"), None),
            ),
            out_specs=(every, every),
            check_vma=False,
        )(vectors, sectors, outcomes, sites, environments)

    return run
```

```python
import functools

import jax
import jax.numpy as jnp
from jax import lax
from jax.experimental import pallas as pl
from jax.experimental.pallas import tpu as pltpu
from jax.sharding import Mesh, PartitionSpec as P

OUTCOMES = 4
ORBITALS = 2
LANES = 128
CHUNKS = 4
MARKS = 16
MESH = pl.DeviceIdType.MESH
F32 = jnp.float32
BF16 = jnp.bfloat16


def kernel(
    sizes,
    vec_ref, sec_ref, out_ref, site_ref, env_ref,
    prob_ref, fin_ref,
    fs0, fr0, fs1, fr1, rs0, rr0, rs1, rr1,
    mark_s, mark_r, prob_s, prob_r,
    site_v, env_in, env_w, amps, hot_t,
    site_sem, fsend, frecv, rsend, rrecv, esend, erecv, msend, mrecv, psend, precv,
):
    n_sec, n_grp, n_own, cap = sizes
    n = n_sec * n_own
    n_row = n_grp * n_own
    samples, width = vec_ref.shape
    depth = env_ref.shape[3]
    blocks = width // LANES
    per_block = LANES // depth
    per_chunk = n // CHUNKS
    rows = per_chunk * cap
    fs, fr, rs, rr = (fs0, fs1), (fr0, fr1), (rs0, rs1), (rr0, rr1)

    si, gi, oi = lax.axis_index("sector"), lax.axis_index("grp"), lax.axis_index("own")
    me = si * n_own + oi
    row_me = gi * n_own + oi

    def peer(pos):
        pos = lax.rem(pos, n)
        return (lax.div(pos, n_own), gi, lax.rem(pos, n_own))

    def row_peer(pos):
        pos = lax.rem(pos, n_row)
        return (si, lax.div(pos, n_own), lax.rem(pos, n_own))

    def loop(low, high, body):
        lax.fori_loop(low, high, lambda i, c: (body(i), c)[1], 0)

    site_copies = [
        pltpu.make_async_copy(site_ref.at[k, oi], site_v.at[k], site_sem.at[k]) for k in range(ORBITALS)
    ]
    for copy in site_copies:
        copy.start()

    barrier = pltpu.get_barrier_semaphore()

    def greet(r):
        pl.semaphore_signal(barrier, inc=1, device_id=peer(me + r), device_id_type=MESH)

    def greet_far(j):
        pl.semaphore_signal(
            barrier,
            inc=1,
            device_id=(si, lax.rem(gi + 1 + lax.div(j, n_own), n_grp), lax.rem(j, n_own)),
            device_id_type=MESH,
        )

    loop(1, n, greet)
    loop(0, (n_grp - 1) * n_own, greet_far)

    def env_part(k, origin, t):
        column = lax.rem(lax.div(origin, per_block) + t, blocks) * LANES
        return env_in.at[
            k, :, pl.ds(pl.multiple_of(origin * depth, depth), depth), pl.ds(pl.multiple_of(column, LANES), LANES)
        ]

    def has_third(origin):
        m = lax.div(origin, per_block)
        return jnp.logical_or(m == 0, m == blocks - 1)

    def env_copy(k, d, t):
        target = row_peer(row_me + d)
        column = lax.rem(lax.div(row_me, per_block) + t, blocks) * LANES
        return pltpu.make_async_remote_copy(
            src_ref=env_ref.at[k, target[2], :, :, pl.ds(pl.multiple_of(column, LANES), LANES)],
            dst_ref=env_part(k, row_me, t),
            send_sem=esend.at[k, d, t],
            recv_sem=erecv.at[k, d, t],
            device_id=target,
            device_id_type=MESH,
        )

    def env_own(k, t):
        column = lax.rem(lax.div(row_me, per_block) + t, blocks) * LANES
        return pltpu.make_async_copy(
            env_ref.at[k, oi, :, :, pl.ds(pl.multiple_of(column, LANES), LANES)],
            env_part(k, row_me, t),
            erecv.at[k, 0, t],
        )

    def env_arrival(k, d, t):
        origin = lax.rem(row_me - d + n_row, n_row)
        part = env_part(k, origin, t)
        return pltpu.make_async_remote_copy(
            src_ref=part,
            dst_ref=part,
            send_sem=esend.at[k, d, t],
            recv_sem=erecv.at[k, d, t],
            device_id=row_peer(row_me + d),
            device_id_type=MESH,
        )

    def env_start(k):
        def one(d):
            env_copy(k, d, 0).start()
            env_copy(k, d, 1).start()

            @pl.when(has_third(row_me))
            def _():
                env_copy(k, d, 2).start()

        env_own(k, 0).start()
        env_own(k, 1).start()

        @pl.when(has_third(row_me))
        def _():
            env_own(k, 2).start()

        loop(1, n_row, one)

    def env_wait(k):
        def one(d):
            env_arrival(k, d, 0).wait_recv()
            env_arrival(k, d, 1).wait_recv()

            @pl.when(has_third(lax.rem(row_me - d + n_row, n_row)))
            def _():
                env_arrival(k, d, 2).wait_recv()

        env_own(k, 0).wait()
        env_own(k, 1).wait()

        @pl.when(has_third(row_me))
        def _():
            env_own(k, 2).wait()

        loop(1, n_row, one)

    def env_sent(k):
        def one(d):
            env_copy(k, d, 0).wait_send()
            env_copy(k, d, 1).wait_send()

            @pl.when(has_third(row_me))
            def _():
                env_copy(k, d, 2).wait_send()

        loop(1, n_row, one)

    def env_build(k):
        for m in range(blocks):
            for t in range(3 if m in (0, blocks - 1) else 2):
                c = (m + t) % blocks
                at = (slice(m * LANES, (m + 1) * LANES), slice(c * LANES, (c + 1) * LANES))
                part = env_in[k, :, at[0], at[1]]
                env_w[:, at[0], at[1]] = part if t == 0 else part + part

    def relative(labels):
        shifted = labels - me
        return jnp.where(shifted < 0, shifted + n, shifted).astype(F32)

    first = lax.broadcasted_iota(jnp.int32, (samples, samples), 0)
    second = lax.broadcasted_iota(jnp.int32, (samples, samples), 1)
    upper = (first < second).astype(F32).astype(BF16)
    slot_rows = []
    slot_columns = []
    marks = jnp.zeros((MARKS, n * LANES), F32)
    mark_row = lax.broadcasted_iota(jnp.int32, (MARKS, samples), 0)
    slot_lane = lax.broadcasted_iota(jnp.int32, (samples, n * LANES), 1).astype(F32)
    for k in range(ORBITALS):
        label = relative(sec_ref[k : k + 1, :])
        hot = (lax.broadcasted_iota(jnp.int32, (n, samples), 0).astype(F32) == label).astype(F32)
        before = jnp.dot(hot.astype(BF16), upper, preferred_element_type=F32)
        place = jnp.sum(before * hot, axis=0, keepdims=True)
        both = [label * cap + place, label * LANES + place]
        columns = [jnp.sum(jnp.where(first == second, row, 0.0), axis=1, keepdims=True) for row in both]
        slot_rows.append(both[0])
        slot_columns.append(columns[0])
        hot_t[k] = (slot_lane == columns[1]).astype(F32).astype(BF16)
        mark = (mark_row == out_ref[k : k + 1, :] + OUTCOMES * k).astype(F32).astype(BF16)
        marks = marks + jnp.dot(mark, hot_t[k], preferred_element_type=F32)
    mark_s[...] = marks.astype(BF16)

    row_at = lax.broadcasted_iota(jnp.int32, (rows, per_chunk * LANES), 0)
    lane_at = lax.broadcasted_iota(jnp.int32, (rows, per_chunk * LANES), 1)
    spread = jnp.zeros((rows, per_chunk * LANES), F32)
    for j in range(per_chunk):
        here = jnp.logical_and(row_at >= j * cap, row_at < (j + 1) * cap)
        same = jnp.logical_and(here, lane_at - j * LANES == row_at - j * cap)
        spread = jnp.where(same, 1.0, spread)
    spread = spread.astype(BF16)

    env_w[...] = jnp.zeros_like(env_w)

    pl.semaphore_wait(barrier, n - 1 + (n_grp - 1) * n_own)

    def piece(ref, r):
        return ref.at[pl.ds(pl.multiple_of(r * 2 * cap, 16), 2 * cap)]

    def tile(ref, r):
        return ref.at[:, pl.ds(pl.multiple_of(r * LANES, LANES), LANES)]

    def mark_copy(r):
        return pltpu.make_async_remote_copy(
            src_ref=tile(mark_s, r),
            dst_ref=tile(mark_r, r),
            send_sem=msend.at[r],
            recv_sem=mrecv.at[r],
            device_id=peer(me + r),
            device_id_type=MESH,
        )

    def prob_copy(r):
        return pltpu.make_async_remote_copy(
            src_ref=tile(prob_s, r),
            dst_ref=tile(prob_r, r),
            send_sem=psend.at[r],
            recv_sem=precv.at[r],
            device_id=peer(me - r + n),
            device_id_type=MESH,
        )

    def out_copy(k, r):
        return pltpu.make_async_remote_copy(
            src_ref=piece(fs[k], r),
            dst_ref=piece(fr[k], r),
            send_sem=fsend.at[k, r],
            recv_sem=frecv.at[k, r],
            device_id=peer(me + r),
            device_id_type=MESH,
        )

    def back_copy(k, r):
        return pltpu.make_async_remote_copy(
            src_ref=piece(rs[k], r),
            dst_ref=piece(rr[k], r),
            send_sem=rsend.at[k, r],
            recv_sem=rrecv.at[k, r],
            device_id=peer(me - r + n),
            device_id_type=MESH,
        )

    def in_chunk(c, act):
        def one(r):
            @pl.when(r > 0)
            def _():
                act(r)

        loop(c * per_chunk, (c + 1) * per_chunk, one)

    def span(c):
        return pl.ds(pl.multiple_of(c * 2 * rows, 16), 2 * rows)

    def tiles(c):
        return pl.ds(pl.multiple_of(c * per_chunk * LANES, LANES), per_chunk * LANES)

    def flat(c):
        return pl.ds(pl.multiple_of(c * rows, 8), rows)

    half = width // 2

    def encode(x):
        parts = [x[:, :half].reshape(per_chunk, 1, cap, half), x[:, half:].reshape(per_chunk, 1, cap, half)]
        return jnp.concatenate(parts, axis=1).reshape(2 * rows, half).astype(BF16)

    def decode(x):
        x = x.astype(F32).reshape(per_chunk, 2, cap, half)
        return jnp.concatenate([x[:, 0].reshape(rows, half), x[:, 1].reshape(rows, half)], axis=1).astype(BF16)

    def first_product(k, c, s, left):
        return jnp.dot(left, site_v[k, :, s * width : (s + 1) * width], preferred_element_type=F32)

    def branch(k, c, amp_of):
        mark = lax.dot_general(
            spread, mark_r[:, tiles(c)], (((1,), (1,)), ((), ())), preferred_element_type=F32
        )
        weights = []
        chosen = []
        picked = jnp.zeros((rows, width), F32)
        for s in range(OUTCOMES):
            amp = amp_of(s)
            image = jnp.dot(amp.astype(BF16), env_w[s], preferred_element_type=F32)
            weights.append(jnp.sum(image * amp, axis=1, keepdims=True))
            at = OUTCOMES * k + s
            chosen.append(mark[:, at : at + 1])
            picked = jnp.where(chosen[s] > 0.0, amp, picked)
        total = weights[0] + weights[1] + weights[2] + weights[3]
        filled = (chosen[0] + chosen[1] + chosen[2] + chosen[3]) > 0.0
        weight = jnp.zeros_like(total)
        for s in range(OUTCOMES):
            weight = jnp.where(chosen[s] > 0.0, weights[s], weight)
        total = jnp.where(filled, total, 1.0)
        scale = lax.rsqrt(jnp.where(filled, weight, 1.0) / width)
        rs[k][span(c), :] = encode(picked * scale)
        in_chunk(c, lambda r: back_copy(k, r).start())
        lanes = lax.broadcasted_iota(jnp.int32, (rows, MARKS), 1)
        probs = jnp.zeros((rows, MARKS), F32)
        for s in range(OUTCOMES):
            value = jnp.where(filled, weights[s] / total, 0.0)
            probs = jnp.where(lanes == OUTCOMES * k + s, value, probs)
        probs = lax.dot_general(
            probs.astype(BF16), spread, (((0,), (0,)), ((), ())), preferred_element_type=F32
        )
        if k == 0:
            prob_s[:, tiles(c)] = probs.astype(BF16)
        else:
            prob_s[:, tiles(c)] = (prob_s[:, tiles(c)].astype(F32) + probs).astype(BF16)
            in_chunk(c, lambda r: prob_copy(r).start())

    current = vec_ref[...]
    for k in range(ORBITALS):

        def pack(c, k=k, current=current):
            place = (lax.broadcasted_iota(jnp.int32, (rows, samples), 0) + c * rows).astype(F32)
            hot = (place == slot_rows[k]).astype(F32).astype(BF16)
            fs[k][span(c), :] = encode(jnp.dot(hot, current, preferred_element_type=F32))
            in_chunk(c, lambda r: out_copy(k, r).start())

        loop(0, CHUNKS, pack)
        fr[k][: 2 * cap] = fs[k][: 2 * cap]
        if k == 0:
            env_start(0)
            loop(1, n, lambda r: mark_copy(r).start())
            mark_r[:, :LANES] = mark_s[:, :LANES]
        site_copies[k].wait()

        def lead(c, k=k):
            in_chunk(c, lambda r: out_copy(k, r).wait_recv())
            left = decode(fr[k][span(c), :])
            for s in range(OUTCOMES):
                amps[flat(c), s * width : (s + 1) * width] = first_product(k, c, s, left)

        def rest(c, k=k):
            branch(k, c, lambda s: amps[flat(c), s * width : (s + 1) * width])

        def work(c, k=k):
            in_chunk(c, lambda r: out_copy(k, r).wait_recv())
            left = decode(fr[k][span(c), :])
            branch(k, c, lambda s: first_product(k, c, s, left))

        if k == 0:
            loop(0, CHUNKS, lead)
            loop(1, n, lambda r: mark_copy(r).wait_recv())
        env_wait(k)
        env_build(k)
        if k == 0:
            env_start(1)
            loop(0, CHUNKS, rest)
        else:
            loop(0, CHUNKS, work)
        rr[k][: 2 * cap] = rs[k][: 2 * cap]

        def gather(c, total, k=k):
            in_chunk(c, lambda r: back_copy(k, r).wait_recv())
            place = (lax.broadcasted_iota(jnp.int32, (samples, rows), 1) + c * rows).astype(F32)
            hot = (place == slot_columns[k]).astype(F32).astype(BF16)
            return total + jnp.dot(hot, decode(rr[k][span(c), :]), preferred_element_type=F32)

        current = lax.fori_loop(0, CHUNKS, gather, jnp.zeros((samples, width), F32)).astype(BF16)
    fin_ref[...] = current
    prob_r[:, :LANES] = prob_s[:, :LANES]
    loop(1, n, lambda r: prob_copy(r).wait_recv())
    tail = prob_r[...]
    side = (((1,), (1,)), ((), ()))
    low = lax.dot_general(tail, hot_t[0], side, preferred_element_type=F32)
    high = lax.dot_general(tail, hot_t[1], side, preferred_element_type=F32)
    prob_ref[...] = jnp.where(mark_row < OUTCOMES, low, high)[: OUTCOMES * ORBITALS].astype(BF16)

    for k in range(ORBITALS):
        loop(1, n, lambda r, k=k: out_copy(k, r).wait_send())
        loop(1, n, lambda r, k=k: back_copy(k, r).wait_send())
        env_sent(k)
    loop(1, n, lambda r: mark_copy(r).wait_send())
    loop(1, n, lambda r: prob_copy(r).wait_send())


def local(sizes, vectors, sectors, outcomes, sites, environments):
    n_sec, n_grp, n_own, cap = sizes
    n, n_row = n_sec * n_own, n_grp * n_own
    samples, width = vectors.shape
    slots = n * cap
    vmem = pl.BlockSpec(memory_space=pltpu.VMEM)
    hbm = pl.BlockSpec(memory_space=pl.ANY)
    dma = pltpu.SemaphoreType.DMA
    halves, tile = pltpu.VMEM((2 * slots, width // 2), BF16), pltpu.VMEM((MARKS, n * LANES), BF16)
    probs, final = pl.pallas_call(
        functools.partial(kernel, sizes),
        out_shape=(
            jax.ShapeDtypeStruct((ORBITALS * OUTCOMES, samples), BF16),
            jax.ShapeDtypeStruct((samples, width), BF16),
        ),
        in_specs=[vmem, vmem, vmem, hbm, hbm],
        out_specs=(vmem, vmem),
        scratch_shapes=[
            halves, halves, halves, halves, halves, halves, halves, halves,
            tile, tile, tile, tile,
            pltpu.VMEM((ORBITALS, width, OUTCOMES * width), BF16),
            pltpu.VMEM((ORBITALS, OUTCOMES, width, width), BF16),
            pltpu.VMEM((OUTCOMES, width, width), BF16),
            pltpu.VMEM((slots, OUTCOMES * width), F32),
            pltpu.VMEM((ORBITALS, samples, n * LANES), BF16),
            dma((ORBITALS,)),
            dma((ORBITALS, n)), dma((ORBITALS, n)), dma((ORBITALS, n)), dma((ORBITALS, n)),
            dma((ORBITALS, n_row, 3)), dma((ORBITALS, n_row, 3)),
            dma((n,)), dma((n,)), dma((n,)), dma((n,)),
        ],
        compiler_params=pltpu.CompilerParams(
            collective_id=0, has_side_effects=True, vmem_limit_bytes=56 * 1024 * 1024
        ),
    )(vectors, sectors.T, outcomes.T, sites, environments)
    return probs.T, final


def solution(mesh):
    def run(vectors, sectors, outcomes, sites, environments):
        sector_size, section_size = mesh.devices.shape
        owners = sites.shape[1] // sector_size
        split = Mesh(
            mesh.devices.reshape(sector_size, section_size // owners, owners), ("sector", "grp", "own")
        )
        every = P(("sector", "grp", "own"), None)
        per_device = vectors.shape[0] // mesh.devices.size
        cap = -(-3 * per_device // sites.shape[1])
        cap = -(-cap // 8) * 8
        return jax.shard_map(
            functools.partial(local, (sector_size, section_size // owners, owners, cap)),
            mesh=split,
            in_specs=(
                every,
                every,
                every,
                P(None, "sector", None, None),
                P(None, "sector", None, ("grp", "own"), None),
            ),
            out_specs=(every, every),
            check_vma=False,
        )(vectors, sectors, outcomes, sites, environments)

    return run
```

```python
import functools

import jax
import jax.numpy as jnp
from jax import lax
from jax.experimental import pallas as pl
from jax.experimental.pallas import tpu as pltpu
from jax.sharding import Mesh, PartitionSpec as P

OUTCOMES = 4
ORBITALS = 2
LANES = 128
CHUNKS = 4
MARKS = 16
MESH = pl.DeviceIdType.MESH
F32 = jnp.float32
BF16 = jnp.bfloat16


def kernel(
    sizes,
    vec_ref, sec_ref, out_ref, site_ref, env_ref,
    prob_ref, fin_ref,
    fs0, fr0, fs1, fr1, rs0, rr0, rs1, rr1,
    mark_s, mark_r, prob_s, prob_r,
    site_v, env_in, env_w, amps, hot_t,
    site_sem, fsend, frecv, rsend, rrecv, esend, erecv, msend, mrecv, psend, precv,
):
    n_sec, n_grp, n_own, cap = sizes
    n = n_sec * n_own
    n_row = n_grp * n_own
    samples, width = vec_ref.shape
    depth = env_ref.shape[3]
    blocks = width // LANES
    per_block = LANES // depth
    per_chunk = n // CHUNKS
    rows = per_chunk * cap
    fs, fr, rs, rr = (fs0, fs1), (fr0, fr1), (rs0, rs1), (rr0, rr1)

    si, gi, oi = lax.axis_index("sector"), lax.axis_index("grp"), lax.axis_index("own")
    me = si * n_own + oi
    row_me = gi * n_own + oi

    def peer(pos):
        pos = lax.rem(pos, n)
        return (lax.div(pos, n_own), gi, lax.rem(pos, n_own))

    def row_peer(pos):
        pos = lax.rem(pos, n_row)
        return (si, lax.div(pos, n_own), lax.rem(pos, n_own))

    def loop(low, high, body):
        lax.fori_loop(low, high, lambda i, c: (body(i), c)[1], 0)

    site_copies = [
        pltpu.make_async_copy(site_ref.at[k, oi], site_v.at[k], site_sem.at[k]) for k in range(ORBITALS)
    ]
    for copy in site_copies:
        copy.start()

    barrier = pltpu.get_barrier_semaphore()

    def greet(r):
        pl.semaphore_signal(barrier, inc=1, device_id=peer(me + r), device_id_type=MESH)

    def greet_far(j):
        pl.semaphore_signal(
            barrier,
            inc=1,
            device_id=(si, lax.rem(gi + 1 + lax.div(j, n_own), n_grp), lax.rem(j, n_own)),
            device_id_type=MESH,
        )

    loop(1, n, greet)
    loop(0, (n_grp - 1) * n_own, greet_far)

    def far(block, home):
        side = jnp.where(home < blocks // 2, block > home, block < home)
        return 2 * jnp.maximum(block - home, home - block) + jnp.where(side, 1, 0)

    def sends(block, c, home):
        return far(block, home) <= far(c, home)

    my_block = lax.div(row_me, per_block)

    def env_part(k, origin, t):
        return env_in.at[
            k, :, pl.ds(pl.multiple_of(origin * depth, depth), depth), pl.ds(t * LANES, LANES)
        ]

    def env_copy(k, d, t):
        target = row_peer(row_me + d)
        return pltpu.make_async_remote_copy(
            src_ref=env_ref.at[k, target[2], :, :, pl.ds(t * LANES, LANES)],
            dst_ref=env_part(k, row_me, t),
            send_sem=esend.at[k, d, t],
            recv_sem=erecv.at[k, d, t],
            device_id=target,
            device_id_type=MESH,
        )

    def env_own(k):
        return pltpu.make_async_copy(
            env_ref.at[k, oi],
            env_in.at[k, :, pl.ds(pl.multiple_of(row_me * depth, depth), depth), :],
            erecv.at[k, 0, 0],
        )

    def env_arrival(k, d, t):
        part = env_part(k, lax.rem(row_me - d + n_row, n_row), t)
        return pltpu.make_async_remote_copy(
            src_ref=part,
            dst_ref=part,
            send_sem=esend.at[k, d, t],
            recv_sem=erecv.at[k, d, t],
            device_id=row_peer(row_me + d),
            device_id_type=MESH,
        )

    def for_sent(d, act):
        home = lax.div(lax.rem(row_me + d, n_row), per_block)
        for t in range(blocks):
            pl.when(sends(my_block, t, home))(functools.partial(act, d, t))

    def for_arriving(d, act):
        origin = lax.div(lax.rem(row_me - d + n_row, n_row), per_block)
        for t in range(blocks):
            pl.when(sends(origin, t, my_block))(functools.partial(act, d, t))

    def env_start(k):
        env_own(k).start()
        loop(1, n_row, lambda d: for_sent(d, lambda d, t: env_copy(k, d, t).start()))

    def env_wait(k):
        env_own(k).wait()
        loop(1, n_row, lambda d: for_arriving(d, lambda d, t: env_arrival(k, d, t).wait_recv()))

    def env_sent(k):
        loop(1, n_row, lambda d: for_sent(d, lambda d, t: env_copy(k, d, t).wait_send()))

    def env_build(k):
        for m in range(blocks):
            for c in range(blocks):

                @pl.when(sends(m, c, my_block))
                def _(m=m, c=c):
                    at = (slice(m * LANES, (m + 1) * LANES), slice(c * LANES, (c + 1) * LANES))
                    part = env_in[k, :, at[0], at[1]]
                    env_w[:, at[0], at[1]] = part if m == c else part + part

    def relative(labels):
        shifted = labels - me
        return jnp.where(shifted < 0, shifted + n, shifted).astype(F32)

    first = lax.broadcasted_iota(jnp.int32, (samples, samples), 0)
    second = lax.broadcasted_iota(jnp.int32, (samples, samples), 1)
    upper = (first < second).astype(F32).astype(BF16)
    slot_rows = []
    slot_columns = []
    marks = jnp.zeros((MARKS, n * LANES), F32)
    mark_row = lax.broadcasted_iota(jnp.int32, (MARKS, samples), 0)
    slot_lane = lax.broadcasted_iota(jnp.int32, (samples, n * LANES), 1).astype(F32)
    for k in range(ORBITALS):
        label = relative(sec_ref[k : k + 1, :])
        hot = (lax.broadcasted_iota(jnp.int32, (n, samples), 0).astype(F32) == label).astype(F32)
        before = jnp.dot(hot.astype(BF16), upper, preferred_element_type=F32)
        place = jnp.sum(before * hot, axis=0, keepdims=True)
        both = [label * cap + place, label * LANES + place]
        columns = [jnp.sum(jnp.where(first == second, row, 0.0), axis=1, keepdims=True) for row in both]
        slot_rows.append(both[0])
        slot_columns.append(columns[0])
        hot_t[k] = (slot_lane == columns[1]).astype(F32).astype(BF16)
        mark = (mark_row == out_ref[k : k + 1, :] + OUTCOMES * k).astype(F32).astype(BF16)
        marks = marks + jnp.dot(mark, hot_t[k], preferred_element_type=F32)
    mark_s[...] = marks.astype(BF16)

    row_at = lax.broadcasted_iota(jnp.int32, (rows, per_chunk * LANES), 0)
    lane_at = lax.broadcasted_iota(jnp.int32, (rows, per_chunk * LANES), 1)
    spread = jnp.zeros((rows, per_chunk * LANES), F32)
    for j in range(per_chunk):
        here = jnp.logical_and(row_at >= j * cap, row_at < (j + 1) * cap)
        same = jnp.logical_and(here, lane_at - j * LANES == row_at - j * cap)
        spread = jnp.where(same, 1.0, spread)
    spread = spread.astype(BF16)

    env_w[...] = jnp.zeros_like(env_w)

    pl.semaphore_wait(barrier, n - 1 + (n_grp - 1) * n_own)

    def piece(ref, r):
        return ref.at[pl.ds(pl.multiple_of(r * 2 * cap, 16), 2 * cap)]

    def tile(ref, r):
        return ref.at[:, pl.ds(pl.multiple_of(r * LANES, LANES), LANES)]

    def mark_copy(r):
        return pltpu.make_async_remote_copy(
            src_ref=tile(mark_s, r),
            dst_ref=tile(mark_r, r),
            send_sem=msend.at[r],
            recv_sem=mrecv.at[r],
            device_id=peer(me + r),
            device_id_type=MESH,
        )

    def prob_copy(r):
        return pltpu.make_async_remote_copy(
            src_ref=tile(prob_s, r),
            dst_ref=tile(prob_r, r),
            send_sem=psend.at[r],
            recv_sem=precv.at[r],
            device_id=peer(me - r + n),
            device_id_type=MESH,
        )

    def out_copy(k, r):
        return pltpu.make_async_remote_copy(
            src_ref=piece(fs[k], r),
            dst_ref=piece(fr[k], r),
            send_sem=fsend.at[k, r],
            recv_sem=frecv.at[k, r],
            device_id=peer(me + r),
            device_id_type=MESH,
        )

    def back_copy(k, r):
        return pltpu.make_async_remote_copy(
            src_ref=piece(rs[k], r),
            dst_ref=piece(rr[k], r),
            send_sem=rsend.at[k, r],
            recv_sem=rrecv.at[k, r],
            device_id=peer(me - r + n),
            device_id_type=MESH,
        )

    def in_chunk(c, act):
        def one(r):
            @pl.when(r > 0)
            def _():
                act(r)

        loop(c * per_chunk, (c + 1) * per_chunk, one)

    def span(c):
        return pl.ds(pl.multiple_of(c * 2 * rows, 16), 2 * rows)

    def tiles(c):
        return pl.ds(pl.multiple_of(c * per_chunk * LANES, LANES), per_chunk * LANES)

    def flat(c):
        return pl.ds(pl.multiple_of(c * rows, 8), rows)

    half = width // 2

    def encode(x):
        parts = [x[:, :half].reshape(per_chunk, 1, cap, half), x[:, half:].reshape(per_chunk, 1, cap, half)]
        return jnp.concatenate(parts, axis=1).reshape(2 * rows, half).astype(BF16)

    def decode(x):
        x = x.astype(F32).reshape(per_chunk, 2, cap, half)
        return jnp.concatenate([x[:, 0].reshape(rows, half), x[:, 1].reshape(rows, half)], axis=1).astype(BF16)

    def first_product(k, c, s, left):
        return jnp.dot(left, site_v[k, :, s * width : (s + 1) * width], preferred_element_type=F32)

    def branch(k, c, amp_of):
        mark = lax.dot_general(
            spread, mark_r[:, tiles(c)], (((1,), (1,)), ((), ())), preferred_element_type=F32
        )
        weights = []
        chosen = []
        picked = jnp.zeros((rows, width), F32)
        for s in range(OUTCOMES):
            amp = amp_of(s)
            image = jnp.dot(amp.astype(BF16), env_w[s], preferred_element_type=F32)
            weights.append(jnp.sum(image * amp, axis=1, keepdims=True))
            at = OUTCOMES * k + s
            chosen.append(mark[:, at : at + 1])
            picked = jnp.where(chosen[s] > 0.0, amp, picked)
        total = weights[0] + weights[1] + weights[2] + weights[3]
        filled = (chosen[0] + chosen[1] + chosen[2] + chosen[3]) > 0.0
        weight = jnp.zeros_like(total)
        for s in range(OUTCOMES):
            weight = jnp.where(chosen[s] > 0.0, weights[s], weight)
        total = jnp.where(filled, total, 1.0)
        scale = lax.rsqrt(jnp.where(filled, weight, 1.0) / width)
        rs[k][span(c), :] = encode(picked * scale)
        in_chunk(c, lambda r: back_copy(k, r).start())
        lanes = lax.broadcasted_iota(jnp.int32, (rows, MARKS), 1)
        probs = jnp.zeros((rows, MARKS), F32)
        for s in range(OUTCOMES):
            value = jnp.where(filled, weights[s] / total, 0.0)
            probs = jnp.where(lanes == OUTCOMES * k + s, value, probs)
        probs = lax.dot_general(
            probs.astype(BF16), spread, (((0,), (0,)), ((), ())), preferred_element_type=F32
        )
        if k == 0:
            prob_s[:, tiles(c)] = probs.astype(BF16)
        else:
            prob_s[:, tiles(c)] = (prob_s[:, tiles(c)].astype(F32) + probs).astype(BF16)
            in_chunk(c, lambda r: prob_copy(r).start())

    current = vec_ref[...]
    for k in range(ORBITALS):

        def pack(c, k=k, current=current):
            place = (lax.broadcasted_iota(jnp.int32, (rows, samples), 0) + c * rows).astype(F32)
            hot = (place == slot_rows[k]).astype(F32).astype(BF16)
            fs[k][span(c), :] = encode(jnp.dot(hot, current, preferred_element_type=F32))
            in_chunk(c, lambda r: out_copy(k, r).start())

        loop(0, CHUNKS, pack)
        fr[k][: 2 * cap] = fs[k][: 2 * cap]
        if k == 0:
            env_start(0)
            loop(1, n, lambda r: mark_copy(r).start())
            mark_r[:, :LANES] = mark_s[:, :LANES]
        site_copies[k].wait()

        def lead(c, k=k):
            in_chunk(c, lambda r: out_copy(k, r).wait_recv())
            left = decode(fr[k][span(c), :])
            for s in range(OUTCOMES):
                amps[flat(c), s * width : (s + 1) * width] = first_product(k, c, s, left)

        def rest(c, k=k):
            branch(k, c, lambda s: amps[flat(c), s * width : (s + 1) * width])

        def work(c, k=k):
            in_chunk(c, lambda r: out_copy(k, r).wait_recv())
            left = decode(fr[k][span(c), :])
            branch(k, c, lambda s: first_product(k, c, s, left))

        if k == 0:
            loop(0, CHUNKS, lead)
            loop(1, n, lambda r: mark_copy(r).wait_recv())
        env_wait(k)
        env_build(k)
        if k == 0:
            env_start(1)
            loop(0, CHUNKS, rest)
        else:
            loop(0, CHUNKS, work)
        rr[k][: 2 * cap] = rs[k][: 2 * cap]

        def gather(c, total, k=k):
            in_chunk(c, lambda r: back_copy(k, r).wait_recv())
            place = (lax.broadcasted_iota(jnp.int32, (samples, rows), 1) + c * rows).astype(F32)
            hot = (place == slot_columns[k]).astype(F32).astype(BF16)
            return total + jnp.dot(hot, decode(rr[k][span(c), :]), preferred_element_type=F32)

        current = lax.fori_loop(0, CHUNKS, gather, jnp.zeros((samples, width), F32)).astype(BF16)
    fin_ref[...] = current
    prob_r[:, :LANES] = prob_s[:, :LANES]
    loop(1, n, lambda r: prob_copy(r).wait_recv())
    tail = prob_r[...]
    side = (((1,), (1,)), ((), ()))
    low = lax.dot_general(tail, hot_t[0], side, preferred_element_type=F32)
    high = lax.dot_general(tail, hot_t[1], side, preferred_element_type=F32)
    prob_ref[...] = jnp.where(mark_row < OUTCOMES, low, high)[: OUTCOMES * ORBITALS].astype(BF16)

    for k in range(ORBITALS):
        loop(1, n, lambda r, k=k: out_copy(k, r).wait_send())
        loop(1, n, lambda r, k=k: back_copy(k, r).wait_send())
        env_sent(k)
    loop(1, n, lambda r: mark_copy(r).wait_send())
    loop(1, n, lambda r: prob_copy(r).wait_send())


def local(sizes, vectors, sectors, outcomes, sites, environments):
    n_sec, n_grp, n_own, cap = sizes
    n, n_row = n_sec * n_own, n_grp * n_own
    samples, width = vectors.shape
    slots = n * cap
    blocks = width // LANES
    vmem = pl.BlockSpec(memory_space=pltpu.VMEM)
    hbm = pl.BlockSpec(memory_space=pl.ANY)
    dma = pltpu.SemaphoreType.DMA
    halves, tile = pltpu.VMEM((2 * slots, width // 2), BF16), pltpu.VMEM((MARKS, n * LANES), BF16)
    probs, final = pl.pallas_call(
        functools.partial(kernel, sizes),
        out_shape=(
            jax.ShapeDtypeStruct((ORBITALS * OUTCOMES, samples), BF16),
            jax.ShapeDtypeStruct((samples, width), BF16),
        ),
        in_specs=[vmem, vmem, vmem, hbm, hbm],
        out_specs=(vmem, vmem),
        scratch_shapes=[
            halves, halves, halves, halves, halves, halves, halves, halves,
            tile, tile, tile, tile,
            pltpu.VMEM((ORBITALS, width, OUTCOMES * width), BF16),
            pltpu.VMEM((ORBITALS, OUTCOMES, width, width), BF16),
            pltpu.VMEM((OUTCOMES, width, width), BF16),
            pltpu.VMEM((slots, OUTCOMES * width), F32),
            pltpu.VMEM((ORBITALS, samples, n * LANES), BF16),
            dma((ORBITALS,)),
            dma((ORBITALS, n)), dma((ORBITALS, n)), dma((ORBITALS, n)), dma((ORBITALS, n)),
            dma((ORBITALS, n_row, blocks)), dma((ORBITALS, n_row, blocks)),
            dma((n,)), dma((n,)), dma((n,)), dma((n,)),
        ],
        compiler_params=pltpu.CompilerParams(
            collective_id=0, has_side_effects=True, vmem_limit_bytes=56 * 1024 * 1024
        ),
    )(vectors, sectors.T, outcomes.T, sites, environments)
    return probs.T, final


def solution(mesh):
    def run(vectors, sectors, outcomes, sites, environments):
        sector_size, section_size = mesh.devices.shape
        owners = sites.shape[1] // sector_size
        split = Mesh(
            mesh.devices.reshape(sector_size, section_size // owners, owners), ("sector", "grp", "own")
        )
        every = P(("sector", "grp", "own"), None)
        per_device = vectors.shape[0] // mesh.devices.size
        cap = -(-3 * per_device // sites.shape[1])
        cap = -(-cap // 8) * 8
        return jax.shard_map(
            functools.partial(local, (sector_size, section_size // owners, owners, cap)),
            mesh=split,
            in_specs=(
                every,
                every,
                every,
                P(None, "sector", None, None),
                P(None, "sector", None, ("grp", "own"), None),
            ),
            out_specs=(every, every),
            check_vma=False,
        )(vectors, sectors, outcomes, sites, environments)

    return run
```

```python
import functools

import jax
import jax.numpy as jnp
from jax import lax
from jax.experimental import pallas as pl
from jax.experimental.pallas import tpu as pltpu
from jax.sharding import Mesh, PartitionSpec as P

OUTCOMES = 4
ORBITALS = 2
LANES = 128
CHUNKS = 4
MARKS = 16
MESH = pl.DeviceIdType.MESH
F32 = jnp.float32
BF16 = jnp.bfloat16


def kernel(
    sizes,
    vec_ref, sec_ref, out_ref, site_ref, env_ref,
    prob_ref, fin_ref,
    fs0, fr0, fs1, fr1, rs0, rr0, rs1, rr1,
    mark_s, mark_r, prob_s, prob_r,
    site_v, env_in, env_w, amps, hot_t,
    site_sem, fsend, frecv, rsend, rrecv, esend, erecv, msend, mrecv, psend, precv,
):
    n_sec, n_grp, n_own, cap = sizes
    n = n_sec * n_own
    n_row = n_grp * n_own
    samples, width = vec_ref.shape
    depth = env_ref.shape[3]
    blocks = width // LANES
    per_block = LANES // depth
    per_chunk = n // CHUNKS
    rows = per_chunk * cap
    fs, fr, rs, rr = (fs0, fs1), (fr0, fr1), (rs0, rs1), (rr0, rr1)

    si, gi, oi = lax.axis_index("sector"), lax.axis_index("grp"), lax.axis_index("own")
    me = si * n_own + oi
    row_me = gi * n_own + oi

    def peer(pos):
        pos = lax.rem(pos, n)
        return (lax.div(pos, n_own), gi, lax.rem(pos, n_own))

    def row_peer(pos):
        pos = lax.rem(pos, n_row)
        return (si, lax.div(pos, n_own), lax.rem(pos, n_own))

    def loop(low, high, body):
        lax.fori_loop(low, high, lambda i, c: (body(i), c)[1], 0)

    site_copies = [
        pltpu.make_async_copy(site_ref.at[k, oi], site_v.at[k], site_sem.at[k]) for k in range(ORBITALS)
    ]
    for copy in site_copies:
        copy.start()

    barrier = pltpu.get_barrier_semaphore()

    def greet(r):
        pl.semaphore_signal(barrier, inc=1, device_id=peer(me + r), device_id_type=MESH)

    def greet_far(j):
        pl.semaphore_signal(
            barrier,
            inc=1,
            device_id=(si, lax.rem(gi + 1 + lax.div(j, n_own), n_grp), lax.rem(j, n_own)),
            device_id_type=MESH,
        )

    loop(1, n, greet)
    loop(0, (n_grp - 1) * n_own, greet_far)

    def far(block, home):
        side = jnp.where(home < blocks // 2, block > home, block < home)
        return 2 * jnp.maximum(block - home, home - block) + jnp.where(side, 1, 0)

    def sends(block, c, home):
        return far(block, home) <= far(c, home)

    my_block = lax.div(row_me, per_block)

    def env_part(k, origin, t):
        return env_in.at[
            k, :, pl.ds(pl.multiple_of(origin * depth, depth), depth), pl.ds(t * LANES, LANES)
        ]

    def env_copy(k, d, t):
        target = row_peer(row_me + d)
        return pltpu.make_async_remote_copy(
            src_ref=env_ref.at[k, target[2], :, :, pl.ds(t * LANES, LANES)],
            dst_ref=env_part(k, row_me, t),
            send_sem=esend.at[k, d, t],
            recv_sem=erecv.at[k, d, t],
            device_id=target,
            device_id_type=MESH,
        )

    def env_own(k):
        return pltpu.make_async_copy(
            env_ref.at[k, oi],
            env_in.at[k, :, pl.ds(pl.multiple_of(row_me * depth, depth), depth), :],
            erecv.at[k, 0, 0],
        )

    def env_arrival(k, d, t):
        part = env_part(k, lax.rem(row_me - d + n_row, n_row), t)
        return pltpu.make_async_remote_copy(
            src_ref=part,
            dst_ref=part,
            send_sem=esend.at[k, d, t],
            recv_sem=erecv.at[k, d, t],
            device_id=row_peer(row_me + d),
            device_id_type=MESH,
        )

    def for_sent(d, act):
        home = lax.div(lax.rem(row_me + d, n_row), per_block)
        for t in range(blocks):
            pl.when(sends(my_block, t, home))(functools.partial(act, d, t))

    def for_arriving(d, act):
        origin = lax.div(lax.rem(row_me - d + n_row, n_row), per_block)
        for t in range(blocks):
            pl.when(sends(origin, t, my_block))(functools.partial(act, d, t))

    def env_start(k):
        env_own(k).start()
        loop(1, n_row, lambda d: for_sent(d, lambda d, t: env_copy(k, d, t).start()))

    def env_wait(k):
        env_own(k).wait()
        loop(1, n_row, lambda d: for_arriving(d, lambda d, t: env_arrival(k, d, t).wait_recv()))

    def env_sent(k):
        loop(1, n_row, lambda d: for_sent(d, lambda d, t: env_copy(k, d, t).wait_send()))

    def env_build(k):
        for m in range(blocks):
            for c in range(blocks):

                @pl.when(sends(m, c, my_block))
                def _(m=m, c=c):
                    at = (slice(m * LANES, (m + 1) * LANES), slice(c * LANES, (c + 1) * LANES))
                    part = env_in[k, :, at[0], at[1]]
                    env_w[:, at[0], at[1]] = part if m == c else part + part

    def relative(labels):
        shifted = labels - me
        return jnp.where(shifted < 0, shifted + n, shifted).astype(F32)

    first = lax.broadcasted_iota(jnp.int32, (samples, samples), 0)
    second = lax.broadcasted_iota(jnp.int32, (samples, samples), 1)
    upper = (first < second).astype(F32).astype(BF16)
    slot_rows = []
    slot_columns = []
    mark_row = lax.broadcasted_iota(jnp.int32, (MARKS, samples), 0)
    wide_columns = []
    for k in range(ORBITALS):
        label = relative(sec_ref[k : k + 1, :])
        hot = (lax.broadcasted_iota(jnp.int32, (n, samples), 0).astype(F32) == label).astype(F32)
        before = jnp.dot(hot.astype(BF16), upper, preferred_element_type=F32)
        place = jnp.sum(before * hot, axis=0, keepdims=True)
        both = [label * cap + place, label * LANES + place]
        columns = [jnp.sum(jnp.where(first == second, row, 0.0), axis=1, keepdims=True) for row in both]
        slot_rows.append(both[0])
        slot_columns.append(columns[0])
        wide_columns.append(columns[1])

    def make_marks():
        marks = jnp.zeros((MARKS, n * LANES), F32)
        slot_lane = lax.broadcasted_iota(jnp.int32, (samples, n * LANES), 1).astype(F32)
        for k in range(ORBITALS):
            hot_t[k] = (slot_lane == wide_columns[k]).astype(F32).astype(BF16)
            mark = (mark_row == out_ref[k : k + 1, :] + OUTCOMES * k).astype(F32).astype(BF16)
            marks = marks + jnp.dot(mark, hot_t[k], preferred_element_type=F32)
        mark_s[...] = marks.astype(BF16)

    pl.semaphore_wait(barrier, n - 1 + (n_grp - 1) * n_own)
    env_start(0)

    row_at = lax.broadcasted_iota(jnp.int32, (rows, per_chunk * LANES), 0)
    lane_at = lax.broadcasted_iota(jnp.int32, (rows, per_chunk * LANES), 1)
    spread = jnp.zeros((rows, per_chunk * LANES), F32)
    for j in range(per_chunk):
        here = jnp.logical_and(row_at >= j * cap, row_at < (j + 1) * cap)
        same = jnp.logical_and(here, lane_at - j * LANES == row_at - j * cap)
        spread = jnp.where(same, 1.0, spread)
    spread = spread.astype(BF16)


    def piece(ref, r):
        return ref.at[pl.ds(pl.multiple_of(r * 2 * cap, 16), 2 * cap)]

    def tile(ref, r):
        return ref.at[:, pl.ds(pl.multiple_of(r * LANES, LANES), LANES)]

    def mark_copy(r):
        return pltpu.make_async_remote_copy(
            src_ref=tile(mark_s, r),
            dst_ref=tile(mark_r, r),
            send_sem=msend.at[r],
            recv_sem=mrecv.at[r],
            device_id=peer(me + r),
            device_id_type=MESH,
        )

    def prob_copy(r):
        return pltpu.make_async_remote_copy(
            src_ref=tile(prob_s, r),
            dst_ref=tile(prob_r, r),
            send_sem=psend.at[r],
            recv_sem=precv.at[r],
            device_id=peer(me - r + n),
            device_id_type=MESH,
        )

    def out_copy(k, r):
        return pltpu.make_async_remote_copy(
            src_ref=piece(fs[k], r),
            dst_ref=piece(fr[k], r),
            send_sem=fsend.at[k, r],
            recv_sem=frecv.at[k, r],
            device_id=peer(me + r),
            device_id_type=MESH,
        )

    def back_copy(k, r):
        return pltpu.make_async_remote_copy(
            src_ref=piece(rs[k], r),
            dst_ref=piece(rr[k], r),
            send_sem=rsend.at[k, r],
            recv_sem=rrecv.at[k, r],
            device_id=peer(me - r + n),
            device_id_type=MESH,
        )

    def in_chunk(c, act):
        def one(r):
            @pl.when(r > 0)
            def _():
                act(r)

        loop(c * per_chunk, (c + 1) * per_chunk, one)

    def span(c):
        return pl.ds(pl.multiple_of(c * 2 * rows, 16), 2 * rows)

    def tiles(c):
        return pl.ds(pl.multiple_of(c * per_chunk * LANES, LANES), per_chunk * LANES)

    def flat(c):
        return pl.ds(pl.multiple_of(c * rows, 8), rows)

    half = width // 2

    def encode(x):
        parts = [x[:, :half].reshape(per_chunk, 1, cap, half), x[:, half:].reshape(per_chunk, 1, cap, half)]
        return jnp.concatenate(parts, axis=1).reshape(2 * rows, half).astype(BF16)

    def decode(x):
        x = x.astype(F32).reshape(per_chunk, 2, cap, half)
        return jnp.concatenate([x[:, 0].reshape(rows, half), x[:, 1].reshape(rows, half)], axis=1).astype(BF16)

    def first_product(k, c, s, left):
        return jnp.dot(left, site_v[k, :, s * width : (s + 1) * width], preferred_element_type=F32)

    def branch(k, c, amp_of):
        mark = lax.dot_general(
            spread, mark_r[:, tiles(c)], (((1,), (1,)), ((), ())), preferred_element_type=F32
        )
        weights = []
        chosen = []
        picked = jnp.zeros((rows, width), F32)
        for s in range(OUTCOMES):
            amp = amp_of(s)
            image = jnp.dot(amp.astype(BF16), env_w[s], preferred_element_type=F32)
            weights.append(jnp.sum(image * amp, axis=1, keepdims=True))
            at = OUTCOMES * k + s
            chosen.append(mark[:, at : at + 1])
            picked = jnp.where(chosen[s] > 0.0, amp, picked)
        total = weights[0] + weights[1] + weights[2] + weights[3]
        filled = (chosen[0] + chosen[1] + chosen[2] + chosen[3]) > 0.0
        weight = jnp.zeros_like(total)
        for s in range(OUTCOMES):
            weight = jnp.where(chosen[s] > 0.0, weights[s], weight)
        total = jnp.where(filled, total, 1.0)
        scale = lax.rsqrt(jnp.where(filled, weight, 1.0) / width)
        rs[k][span(c), :] = encode(picked * scale)
        in_chunk(c, lambda r: back_copy(k, r).start())
        lanes = lax.broadcasted_iota(jnp.int32, (rows, MARKS), 1)
        probs = jnp.zeros((rows, MARKS), F32)
        for s in range(OUTCOMES):
            value = jnp.where(filled, weights[s] / total, 0.0)
            probs = jnp.where(lanes == OUTCOMES * k + s, value, probs)
        probs = lax.dot_general(
            probs.astype(BF16), spread, (((0,), (0,)), ((), ())), preferred_element_type=F32
        )
        if k == 0:
            prob_s[:, tiles(c)] = probs.astype(BF16)
        else:
            prob_s[:, tiles(c)] = (prob_s[:, tiles(c)].astype(F32) + probs).astype(BF16)
            in_chunk(c, lambda r: prob_copy(r).start())

    current = vec_ref[...]
    for k in range(ORBITALS):

        def pack(c, k=k, current=current):
            place = (lax.broadcasted_iota(jnp.int32, (rows, samples), 0) + c * rows).astype(F32)
            hot = (place == slot_rows[k]).astype(F32).astype(BF16)
            fs[k][span(c), :] = encode(jnp.dot(hot, current, preferred_element_type=F32))
            in_chunk(c, lambda r: out_copy(k, r).start())

        loop(0, CHUNKS, pack)
        fr[k][: 2 * cap] = fs[k][: 2 * cap]
        if k == 0:
            env_w[...] = jnp.zeros_like(env_w)
            make_marks()
            loop(1, n, lambda r: mark_copy(r).start())
            mark_r[:, :LANES] = mark_s[:, :LANES]
        site_copies[k].wait()

        def lead(c, k=k):
            in_chunk(c, lambda r: out_copy(k, r).wait_recv())
            left = decode(fr[k][span(c), :])
            for s in range(OUTCOMES):
                amps[flat(c), s * width : (s + 1) * width] = first_product(k, c, s, left)

        def rest(c, k=k):
            branch(k, c, lambda s: amps[flat(c), s * width : (s + 1) * width])

        def work(c, k=k):
            in_chunk(c, lambda r: out_copy(k, r).wait_recv())
            left = decode(fr[k][span(c), :])
            branch(k, c, lambda s: first_product(k, c, s, left))

        if k == 0:
            loop(0, CHUNKS, lead)
            loop(1, n, lambda r: mark_copy(r).wait_recv())
        env_wait(k)
        env_build(k)
        if k == 0:
            env_start(1)
            loop(0, CHUNKS, rest)
        else:
            loop(0, CHUNKS, work)
        rr[k][: 2 * cap] = rs[k][: 2 * cap]

        def gather(c, total, k=k):
            in_chunk(c, lambda r: back_copy(k, r).wait_recv())
            place = (lax.broadcasted_iota(jnp.int32, (samples, rows), 1) + c * rows).astype(F32)
            hot = (place == slot_columns[k]).astype(F32).astype(BF16)
            return total + jnp.dot(hot, decode(rr[k][span(c), :]), preferred_element_type=F32)

        current = lax.fori_loop(0, CHUNKS, gather, jnp.zeros((samples, width), F32)).astype(BF16)
    fin_ref[...] = current
    prob_r[:, :LANES] = prob_s[:, :LANES]
    loop(1, n, lambda r: prob_copy(r).wait_recv())
    tail = prob_r[...]
    side = (((1,), (1,)), ((), ()))
    low = lax.dot_general(tail, hot_t[0], side, preferred_element_type=F32)
    high = lax.dot_general(tail, hot_t[1], side, preferred_element_type=F32)
    prob_ref[...] = jnp.where(mark_row < OUTCOMES, low, high)[: OUTCOMES * ORBITALS].astype(BF16)

    for k in range(ORBITALS):
        loop(1, n, lambda r, k=k: out_copy(k, r).wait_send())
        loop(1, n, lambda r, k=k: back_copy(k, r).wait_send())
        env_sent(k)
    loop(1, n, lambda r: mark_copy(r).wait_send())
    loop(1, n, lambda r: prob_copy(r).wait_send())


def local(sizes, vectors, sectors, outcomes, sites, environments):
    n_sec, n_grp, n_own, cap = sizes
    n, n_row = n_sec * n_own, n_grp * n_own
    samples, width = vectors.shape
    slots = n * cap
    blocks = width // LANES
    vmem = pl.BlockSpec(memory_space=pltpu.VMEM)
    hbm = pl.BlockSpec(memory_space=pl.ANY)
    dma = pltpu.SemaphoreType.DMA
    halves, tile = pltpu.VMEM((2 * slots, width // 2), BF16), pltpu.VMEM((MARKS, n * LANES), BF16)
    probs, final = pl.pallas_call(
        functools.partial(kernel, sizes),
        out_shape=(
            jax.ShapeDtypeStruct((ORBITALS * OUTCOMES, samples), BF16),
            jax.ShapeDtypeStruct((samples, width), BF16),
        ),
        in_specs=[vmem, vmem, vmem, hbm, hbm],
        out_specs=(vmem, vmem),
        scratch_shapes=[
            halves, halves, halves, halves, halves, halves, halves, halves,
            tile, tile, tile, tile,
            pltpu.VMEM((ORBITALS, width, OUTCOMES * width), BF16),
            pltpu.VMEM((ORBITALS, OUTCOMES, width, width), BF16),
            pltpu.VMEM((OUTCOMES, width, width), BF16),
            pltpu.VMEM((slots, OUTCOMES * width), F32),
            pltpu.VMEM((ORBITALS, samples, n * LANES), BF16),
            dma((ORBITALS,)),
            dma((ORBITALS, n)), dma((ORBITALS, n)), dma((ORBITALS, n)), dma((ORBITALS, n)),
            dma((ORBITALS, n_row, blocks)), dma((ORBITALS, n_row, blocks)),
            dma((n,)), dma((n,)), dma((n,)), dma((n,)),
        ],
        compiler_params=pltpu.CompilerParams(
            collective_id=0, has_side_effects=True, vmem_limit_bytes=56 * 1024 * 1024
        ),
    )(vectors, sectors.T, outcomes.T, sites, environments)
    return probs.T, final


def solution(mesh):
    def run(vectors, sectors, outcomes, sites, environments):
        sector_size, section_size = mesh.devices.shape
        owners = sites.shape[1] // sector_size
        split = Mesh(
            mesh.devices.reshape(sector_size, section_size // owners, owners), ("sector", "grp", "own")
        )
        every = P(("sector", "grp", "own"), None)
        per_device = vectors.shape[0] // mesh.devices.size
        cap = -(-3 * per_device // sites.shape[1])
        cap = -(-cap // 8) * 8
        return jax.shard_map(
            functools.partial(local, (sector_size, section_size // owners, owners, cap)),
            mesh=split,
            in_specs=(
                every,
                every,
                every,
                P(None, "sector", None, None),
                P(None, "sector", None, ("grp", "own"), None),
            ),
            out_specs=(every, every),
            check_vma=False,
        )(vectors, sectors, outcomes, sites, environments)

    return run
```

```python
import functools

import jax
import jax.numpy as jnp
from jax import lax
from jax.experimental import pallas as pl
from jax.experimental.pallas import tpu as pltpu
from jax.sharding import Mesh, PartitionSpec as P

OUTCOMES = 4
ORBITALS = 2
LANES = 128
CHUNKS = 4
MARKS = 16
MESH = pl.DeviceIdType.MESH
F32 = jnp.float32
BF16 = jnp.bfloat16


def kernel(
    sizes,
    vec_ref, sec_ref, out_ref, site_ref, env_ref,
    prob_ref, fin_ref,
    fs0, fr0, fs1, fr1, rs0, rr0, rs1, rr1,
    mark_s, mark_r, prob_s, prob_r,
    site_v, env_in, env_w, amps, hot_t,
    site_sem, fsend, frecv, rsend, rrecv, esend, erecv, msend, mrecv, psend, precv,
):
    n_sec, n_grp, n_own, cap = sizes
    n = n_sec * n_own
    n_row = n_grp * n_own
    samples, width = vec_ref.shape
    depth = env_ref.shape[3]
    blocks = width // LANES
    per_block = LANES // depth
    per_chunk = n // CHUNKS
    rows = per_chunk * cap
    fs, fr, rs, rr = (fs0, fs1), (fr0, fr1), (rs0, rs1), (rr0, rr1)

    si, gi, oi = lax.axis_index("sector"), lax.axis_index("grp"), lax.axis_index("own")
    me = si * n_own + oi
    row_me = gi * n_own + oi

    def peer(pos):
        pos = lax.rem(pos, n)
        return (lax.div(pos, n_own), gi, lax.rem(pos, n_own))

    def row_peer(pos):
        pos = lax.rem(pos, n_row)
        return (si, lax.div(pos, n_own), lax.rem(pos, n_own))

    def loop(low, high, body):
        lax.fori_loop(low, high, lambda i, c: (body(i), c)[1], 0)

    site_copies = [
        pltpu.make_async_copy(site_ref.at[k, oi], site_v.at[k], site_sem.at[k]) for k in range(ORBITALS)
    ]
    for copy in site_copies:
        copy.start()

    barrier = pltpu.get_barrier_semaphore()

    def greet(r):
        pl.semaphore_signal(barrier, inc=1, device_id=peer(me + r), device_id_type=MESH)

    def greet_far(j):
        pl.semaphore_signal(
            barrier,
            inc=1,
            device_id=(si, lax.rem(gi + 1 + lax.div(j, n_own), n_grp), lax.rem(j, n_own)),
            device_id_type=MESH,
        )

    loop(1, n, greet)
    loop(0, (n_grp - 1) * n_own, greet_far)

    def far(block, home):
        side = jnp.where(home < blocks // 2, block > home, block < home)
        return 2 * jnp.maximum(block - home, home - block) + jnp.where(side, 1, 0)

    def sends(block, c, home):
        return far(block, home) <= far(c, home)

    my_block = lax.div(row_me, per_block)

    def env_part(k, origin, t):
        return env_in.at[
            k, :, pl.ds(pl.multiple_of(origin * depth, depth), depth), pl.ds(t * LANES, LANES)
        ]

    def env_copy(k, d, t):
        target = row_peer(row_me + d)
        return pltpu.make_async_remote_copy(
            src_ref=env_ref.at[k, target[2], :, :, pl.ds(t * LANES, LANES)],
            dst_ref=env_part(k, row_me, t),
            send_sem=esend.at[k, d, t],
            recv_sem=erecv.at[k, d, t],
            device_id=target,
            device_id_type=MESH,
        )

    def env_own(k):
        return pltpu.make_async_copy(
            env_ref.at[k, oi],
            env_in.at[k, :, pl.ds(pl.multiple_of(row_me * depth, depth), depth), :],
            erecv.at[k, 0, 0],
        )

    def env_arrival(k, d, t):
        part = env_part(k, lax.rem(row_me - d + n_row, n_row), t)
        return pltpu.make_async_remote_copy(
            src_ref=part,
            dst_ref=part,
            send_sem=esend.at[k, d, t],
            recv_sem=erecv.at[k, d, t],
            device_id=row_peer(row_me + d),
            device_id_type=MESH,
        )

    def for_sent(d, act):
        home = lax.div(lax.rem(row_me + d, n_row), per_block)
        for t in range(blocks):
            pl.when(sends(my_block, t, home))(functools.partial(act, d, t))

    def for_arriving(d, act):
        origin = lax.div(lax.rem(row_me - d + n_row, n_row), per_block)
        for t in range(blocks):
            pl.when(sends(origin, t, my_block))(functools.partial(act, d, t))

    def env_start(k):
        env_own(k).start()
        loop(1, n_row, lambda d: for_sent(d, lambda d, t: env_copy(k, d, t).start()))

    def env_wait(k):
        env_own(k).wait()
        loop(1, n_row, lambda d: for_arriving(d, lambda d, t: env_arrival(k, d, t).wait_recv()))

    def env_sent(k):
        loop(1, n_row, lambda d: for_sent(d, lambda d, t: env_copy(k, d, t).wait_send()))

    def env_build(k):
        for m in range(blocks):
            for c in range(blocks):

                @pl.when(sends(m, c, my_block))
                def _(m=m, c=c):
                    at = (slice(m * LANES, (m + 1) * LANES), slice(c * LANES, (c + 1) * LANES))
                    part = env_in[k, :, at[0], at[1]]
                    env_w[:, at[0], at[1]] = part if m == c else part + part

    def relative(labels):
        shifted = labels - me
        return jnp.where(shifted < 0, shifted + n, shifted).astype(F32)

    first = lax.broadcasted_iota(jnp.int32, (samples, samples), 0)
    second = lax.broadcasted_iota(jnp.int32, (samples, samples), 1)
    upper = (first < second).astype(F32).astype(BF16)
    slot_rows = []
    slot_columns = []
    mark_row = lax.broadcasted_iota(jnp.int32, (MARKS, samples), 0)
    wide_columns = []
    for k in range(ORBITALS):
        label = relative(sec_ref[k : k + 1, :])
        hot = (lax.broadcasted_iota(jnp.int32, (n, samples), 0).astype(F32) == label).astype(F32)
        before = jnp.dot(hot.astype(BF16), upper, preferred_element_type=F32)
        place = jnp.sum(before * hot, axis=0, keepdims=True)
        both = [label * cap + place, label * LANES + place]
        columns = [jnp.sum(jnp.where(first == second, row, 0.0), axis=1, keepdims=True) for row in both]
        slot_rows.append(both[0])
        slot_columns.append(columns[0])
        wide_columns.append(columns[1])

    def make_marks():
        marks = jnp.zeros((MARKS, n * LANES), F32)
        slot_lane = lax.broadcasted_iota(jnp.int32, (samples, n * LANES), 1).astype(F32)
        for k in range(ORBITALS):
            hot_t[k] = (slot_lane == wide_columns[k]).astype(F32).astype(BF16)
            mark = (mark_row == out_ref[k : k + 1, :] + OUTCOMES * k).astype(F32).astype(BF16)
            marks = marks + jnp.dot(mark, hot_t[k], preferred_element_type=F32)
        mark_s[...] = marks.astype(BF16)

    pl.semaphore_wait(barrier, n - 1 + (n_grp - 1) * n_own)
    env_start(0)

    row_at = lax.broadcasted_iota(jnp.int32, (rows, per_chunk * LANES), 0)
    lane_at = lax.broadcasted_iota(jnp.int32, (rows, per_chunk * LANES), 1)
    spread = jnp.zeros((rows, per_chunk * LANES), F32)
    for j in range(per_chunk):
        here = jnp.logical_and(row_at >= j * cap, row_at < (j + 1) * cap)
        same = jnp.logical_and(here, lane_at - j * LANES == row_at - j * cap)
        spread = jnp.where(same, 1.0, spread)
    spread = spread.astype(BF16)


    def piece(ref, r):
        return ref.at[pl.ds(pl.multiple_of(r * 2 * cap, 16), 2 * cap)]

    def tile(ref, r):
        return ref.at[:, pl.ds(pl.multiple_of(r * LANES, LANES), LANES)]

    def mark_copy(r):
        return pltpu.make_async_remote_copy(
            src_ref=tile(mark_s, r),
            dst_ref=tile(mark_r, r),
            send_sem=msend.at[r],
            recv_sem=mrecv.at[r],
            device_id=peer(me + r),
            device_id_type=MESH,
        )

    def prob_copy(r):
        return pltpu.make_async_remote_copy(
            src_ref=tile(prob_s, r),
            dst_ref=tile(prob_r, r),
            send_sem=psend.at[r],
            recv_sem=precv.at[r],
            device_id=peer(me - r + n),
            device_id_type=MESH,
        )

    def out_copy(k, r):
        return pltpu.make_async_remote_copy(
            src_ref=piece(fs[k], r),
            dst_ref=piece(fr[k], r),
            send_sem=fsend.at[k, r],
            recv_sem=frecv.at[k, r],
            device_id=peer(me + r),
            device_id_type=MESH,
        )

    def back_copy(k, r):
        return pltpu.make_async_remote_copy(
            src_ref=piece(rs[k], r),
            dst_ref=piece(rr[k], r),
            send_sem=rsend.at[k, r],
            recv_sem=rrecv.at[k, r],
            device_id=peer(me - r + n),
            device_id_type=MESH,
        )

    def in_chunk(c, act):
        def one(r):
            @pl.when(r > 0)
            def _():
                act(r)

        loop(c * per_chunk, (c + 1) * per_chunk, one)

    def span(c):
        return pl.ds(pl.multiple_of(c * 2 * rows, 16), 2 * rows)

    def tiles(c):
        return pl.ds(pl.multiple_of(c * per_chunk * LANES, LANES), per_chunk * LANES)

    def flat(c):
        return pl.ds(pl.multiple_of(c * rows, 8), rows)

    half = width // 2

    def encode(x):
        parts = [x[:, :half].reshape(per_chunk, 1, cap, half), x[:, half:].reshape(per_chunk, 1, cap, half)]
        return jnp.concatenate(parts, axis=1).reshape(2 * rows, half).astype(BF16)

    def decode(x):
        x = x.astype(F32).reshape(per_chunk, 2, cap, half)
        return jnp.concatenate([x[:, 0].reshape(rows, half), x[:, 1].reshape(rows, half)], axis=1).astype(BF16)

    def first_product(k, c, s, left):
        return jnp.dot(left, site_v[k, :, s * width : (s + 1) * width], preferred_element_type=F32)

    def branch(k, c, amp_of):
        mark = lax.dot_general(
            spread, mark_r[:, tiles(c)], (((1,), (1,)), ((), ())), preferred_element_type=F32
        )
        weights = []
        chosen = []
        picked = jnp.zeros((rows, width), F32)
        for s in range(OUTCOMES):
            amp = amp_of(s)
            image = jnp.dot(amp.astype(BF16), env_w[s], preferred_element_type=F32)
            weights.append(jnp.sum(image * amp, axis=1, keepdims=True))
            at = OUTCOMES * k + s
            chosen.append(mark[:, at : at + 1])
            picked = jnp.where(chosen[s] > 0.0, amp, picked)
        total = weights[0] + weights[1] + weights[2] + weights[3]
        filled = (chosen[0] + chosen[1] + chosen[2] + chosen[3]) > 0.0
        weight = jnp.zeros_like(total)
        for s in range(OUTCOMES):
            weight = jnp.where(chosen[s] > 0.0, weights[s], weight)
        total = jnp.where(filled, total, 1.0)
        scale = lax.rsqrt(jnp.where(filled, weight, 1.0) / width)
        rs[k][span(c), :] = encode(picked * scale)
        in_chunk(c, lambda r: back_copy(k, r).start())
        lanes = lax.broadcasted_iota(jnp.int32, (rows, MARKS), 1)
        probs = jnp.zeros((rows, MARKS), F32)
        for s in range(OUTCOMES):
            value = jnp.where(filled, weights[s] / total, 0.0)
            probs = jnp.where(lanes == OUTCOMES * k + s, value, probs)
        probs = lax.dot_general(
            probs.astype(BF16), spread, (((0,), (0,)), ((), ())), preferred_element_type=F32
        )
        if k == 0:
            prob_s[:, tiles(c)] = probs.astype(BF16)
        else:
            prob_s[:, tiles(c)] = (prob_s[:, tiles(c)].astype(F32) + probs).astype(BF16)
            in_chunk(c, lambda r: prob_copy(r).start())

    current = vec_ref[...]
    for k in range(ORBITALS):

        def pack(c, k=k, current=current):
            place = (lax.broadcasted_iota(jnp.int32, (rows, samples), 0) + c * rows).astype(F32)
            hot = (place == slot_rows[k]).astype(F32).astype(BF16)
            fs[k][span(c), :] = encode(jnp.dot(hot, current, preferred_element_type=F32))
            in_chunk(c, lambda r: out_copy(k, r).start())

        loop(0, CHUNKS, pack)
        fr[k][: 2 * cap] = fs[k][: 2 * cap]
        if k == 0:
            env_w[...] = jnp.zeros_like(env_w)
            make_marks()
            loop(1, n, lambda r: mark_copy(r).start())
            mark_r[:, :LANES] = mark_s[:, :LANES]
        site_copies[k].wait()

        def lead(c, k=k):
            in_chunk(c, lambda r: out_copy(k, r).wait_recv())
            left = decode(fr[k][span(c), :])
            for s in range(OUTCOMES):
                amps[flat(c), s * width : (s + 1) * width] = first_product(k, c, s, left)

        def rest(c, k=k):
            branch(k, c, lambda s: amps[flat(c), s * width : (s + 1) * width])

        def work(c, k=k):
            in_chunk(c, lambda r: out_copy(k, r).wait_recv())
            left = decode(fr[k][span(c), :])
            branch(k, c, lambda s: first_product(k, c, s, left))

        if k == 0:
            loop(0, CHUNKS // 2, lead)
            loop(1, n, lambda r: mark_copy(r).wait_recv())
        env_wait(k)
        env_build(k)
        if k == 0:
            env_start(1)
            loop(0, CHUNKS // 2, rest)
        loop(CHUNKS // 2 if k == 0 else 0, CHUNKS, work)
        rr[k][: 2 * cap] = rs[k][: 2 * cap]

        def gather(c, total, k=k):
            in_chunk(c, lambda r: back_copy(k, r).wait_recv())
            place = (lax.broadcasted_iota(jnp.int32, (samples, rows), 1) + c * rows).astype(F32)
            hot = (place == slot_columns[k]).astype(F32).astype(BF16)
            return total + jnp.dot(hot, decode(rr[k][span(c), :]), preferred_element_type=F32)

        current = lax.fori_loop(0, CHUNKS, gather, jnp.zeros((samples, width), F32)).astype(BF16)
    fin_ref[...] = current
    prob_r[:, :LANES] = prob_s[:, :LANES]
    loop(1, n, lambda r: prob_copy(r).wait_recv())
    tail = prob_r[...]
    side = (((1,), (1,)), ((), ()))
    low = lax.dot_general(tail, hot_t[0], side, preferred_element_type=F32)
    high = lax.dot_general(tail, hot_t[1], side, preferred_element_type=F32)
    prob_ref[...] = jnp.where(mark_row < OUTCOMES, low, high)[: OUTCOMES * ORBITALS].astype(BF16)

    for k in range(ORBITALS):
        loop(1, n, lambda r, k=k: out_copy(k, r).wait_send())
        loop(1, n, lambda r, k=k: back_copy(k, r).wait_send())
        env_sent(k)
    loop(1, n, lambda r: mark_copy(r).wait_send())
    loop(1, n, lambda r: prob_copy(r).wait_send())


def local(sizes, vectors, sectors, outcomes, sites, environments):
    n_sec, n_grp, n_own, cap = sizes
    n, n_row = n_sec * n_own, n_grp * n_own
    samples, width = vectors.shape
    slots = n * cap
    blocks = width // LANES
    vmem = pl.BlockSpec(memory_space=pltpu.VMEM)
    hbm = pl.BlockSpec(memory_space=pl.ANY)
    dma = pltpu.SemaphoreType.DMA
    halves, tile = pltpu.VMEM((2 * slots, width // 2), BF16), pltpu.VMEM((MARKS, n * LANES), BF16)
    probs, final = pl.pallas_call(
        functools.partial(kernel, sizes),
        out_shape=(
            jax.ShapeDtypeStruct((ORBITALS * OUTCOMES, samples), BF16),
            jax.ShapeDtypeStruct((samples, width), BF16),
        ),
        in_specs=[vmem, vmem, vmem, hbm, hbm],
        out_specs=(vmem, vmem),
        scratch_shapes=[
            halves, halves, halves, halves, halves, halves, halves, halves,
            tile, tile, tile, tile,
            pltpu.VMEM((ORBITALS, width, OUTCOMES * width), BF16),
            pltpu.VMEM((ORBITALS, OUTCOMES, width, width), BF16),
            pltpu.VMEM((OUTCOMES, width, width), BF16),
            pltpu.VMEM((slots, OUTCOMES * width), F32),
            pltpu.VMEM((ORBITALS, samples, n * LANES), BF16),
            dma((ORBITALS,)),
            dma((ORBITALS, n)), dma((ORBITALS, n)), dma((ORBITALS, n)), dma((ORBITALS, n)),
            dma((ORBITALS, n_row, blocks)), dma((ORBITALS, n_row, blocks)),
            dma((n,)), dma((n,)), dma((n,)), dma((n,)),
        ],
        compiler_params=pltpu.CompilerParams(
            collective_id=0, has_side_effects=True, vmem_limit_bytes=56 * 1024 * 1024
        ),
    )(vectors, sectors.T, outcomes.T, sites, environments)
    return probs.T, final


def solution(mesh):
    def run(vectors, sectors, outcomes, sites, environments):
        sector_size, section_size = mesh.devices.shape
        owners = sites.shape[1] // sector_size
        split = Mesh(
            mesh.devices.reshape(sector_size, section_size // owners, owners), ("sector", "grp", "own")
        )
        every = P(("sector", "grp", "own"), None)
        per_device = vectors.shape[0] // mesh.devices.size
        cap = -(-3 * per_device // sites.shape[1])
        cap = -(-cap // 8) * 8
        return jax.shard_map(
            functools.partial(local, (sector_size, section_size // owners, owners, cap)),
            mesh=split,
            in_specs=(
                every,
                every,
                every,
                P(None, "sector", None, None),
                P(None, "sector", None, ("grp", "own"), None),
            ),
            out_specs=(every, every),
            check_vma=False,
        )(vectors, sectors, outcomes, sites, environments)

    return run
```
